128 devices in a mesh: section: 2 (over x_lo), dp: 16 (over x_hi, z, core), tensor: 4 (over y).
Axes of the slice: x: 4 (x_hi: 2, x_lo: 2; x = x_hi * 2 + x_lo), y: 4, z: 4, core: 2. Of those that a mesh axis runs over, the one named last changes fastest.
Arguments:
- tokens: bfloat16 [32, 256, 1536], P('dp', 'tensor'), may hold values from -6 to 6
- cotangent: bfloat16 [32, 256, 1536], P('dp', 'tensor'), may hold values from -6 to 6
- route_experts: int32 [2, 32, 256, 6], P('section', 'dp'), may hold values from 0 to 15, as said below
- route_slots: int32 [2, 32, 256, 6], P('section', 'dp'), may hold values from 0 to 127, as said below
- gain_attn: bfloat16 [2, 1536], P('section', ('dp', 'tensor')), may hold values from 0.5 to 1.5
- w_query: bfloat16 [2, 1536, 1536], P('section', 'dp', 'tensor'), may hold values from -0.15625 to 0.15625
- w_key: bfloat16 [2, 1536, 512], P('section', 'dp', 'tensor'), may hold values from -0.15625 to 0.15625
- w_value: bfloat16 [2, 1536, 512], P('section', 'dp', 'tensor'), may hold values from -0.15625 to 0.15625
- w_out: bfloat16 [2, 1536, 1536], P('section', 'tensor', 'dp'), may hold values from -0.625 to 0.625
- gain_ffn: bfloat16 [2, 1536], P('section', ('dp', 'tensor')), may hold values from 0.5 to 1.5
- w_router: bfloat16 [2, 1536, 16], P('section', ('dp', 'tensor')), may hold values from -0.078125 to 0.078125
- w_shared_in: bfloat16 [2, 1536, 2, 1024], P('section', 'dp', None, 'tensor'), may hold values from -0.15625 to 0.15625
- w_shared_down: bfloat16 [2, 1024, 1536], P('section', 'tensor', 'dp'), may hold values from -0.25 to 0.25
- w_expert_in: bfloat16 [2, 1536, 16, 2, 512], P('section', 'dp', None, None, 'tensor'), may hold values from -0.15625 to 0.15625
- w_expert_down: bfloat16 [2, 16, 512, 1536], P('section', None, 'tensor', 'dp'), may hold values from -0.75 to 0.75
Outputs:
- layer_out: bfloat16 [2, 32, 256, 1536], P('section', 'dp', 'tensor')
- layer_in_grad: bfloat16 [2, 32, 256, 1536], P('section', 'dp', 'tensor')
- grad_gain_attn: float32 [2, 1536], P('section', ('dp', 'tensor'))
- grad_query: float32 [2, 1536, 1536], P('section', 'dp', 'tensor')
- grad_key: float32 [2, 1536, 512], P('section', 'dp', 'tensor')
- grad_value: float32 [2, 1536, 512], P('section', 'dp', 'tensor')
- grad_out: float32 [2, 1536, 1536], P('section', 'tensor', 'dp')
- grad_gain_ffn: float32 [2, 1536], P('section', ('dp', 'tensor'))
- grad_router: float32 [2, 1536, 16], P('section', ('dp', 'tensor'))
- grad_shared_in: float32 [2, 1536, 2, 1024], P('section', 'dp', None, 'tensor')
- grad_shared_down: float32 [2, 1024, 1536], P('section', 'tensor', 'dp')
- grad_expert_in: float32 [2, 1536, 16, 2, 512], P('section', 'dp', None, None, 'tensor')
- grad_expert_down: float32 [2, 16, 512, 1536], P('section', None, 'tensor', 'dp')
The draws below stay inside these ranges and needn't reach their ends.
Inputs may be any that keep to these rules, and one draw needn't show every extreme that they name: `route_experts`: in each layer and sequence a token names 6 different experts; every expert is named by 96 - 96 // 3 to 128 tokens of the sequence, and in every sequence some expert by exactly 128. `route_slots`: in each layer and sequence the slots of an expert's routes are 0 to its number of routes - 1, each once.
All inputs are finite; a program needn't handle non-finite values.
Results may differ from the reference program's by a relative error of at most 0.035.
Values may be sent and summed in bfloat16 or wider, within the bound.
No kernel may reach another device: no remote copies, remote signals or barrier semaphores. Data moves between devices by JAX's collectives and lax.ppermute only.
A program may use at most 320 MiB of HBM per device.

```python
import jax
import jax.numpy as jnp
from jax import lax

D = 1536
HQ = 12
HK = 4
HD = 128
FFE = 512
FFS = 1024
TOPK = 6
E = 16
MICRO = 2
LEN = 256
SEQS = 32
LAYERS = 2
AVG = 96
CAP = 128


def route_group(group_key):
    pair_key, spread_key, token_key = jax.random.split(group_key, 3)
    pairing = jax.random.permutation(pair_key, E).astype(jnp.int32)
    spreads = jax.random.randint(spread_key, (E // 2,), 0, AVG // 3 + 1).astype(jnp.int32)
    spreads = spreads.at[0].set(AVG // 3)
    expert_loads = jnp.zeros((E,), jnp.int32)
    expert_loads = expert_loads.at[pairing[0::2]].set(AVG + spreads).at[pairing[1::2]].set(AVG - spreads)
    run_ends = jnp.cumsum(expert_loads).astype(jnp.int32)
    run_starts = run_ends - expert_loads
    positions = jnp.arange(LEN * TOPK, dtype=jnp.int32)
    owners_of = jnp.sum((run_ends[None, :] <= positions[:, None]).astype(jnp.int32), axis=1)
    within_run = positions - run_starts[owners_of]
    shuffle = jax.random.permutation(token_key, LEN).astype(jnp.int32)
    route_place = shuffle[:, None] + LEN * jnp.arange(TOPK, dtype=jnp.int32)[None, :]
    return (owners_of[route_place], within_run[route_place])


def route_tables(base_key):
    group_keys = jax.random.split(base_key, LAYERS * SEQS)
    owners_all, slots_all = jax.vmap(route_group)(group_keys)
    return (owners_all.reshape(LAYERS, SEQS, LEN, TOPK), slots_all.reshape(LAYERS, SEQS, LEN, TOPK))


def draw_route_experts(key, part):
    tables = route_tables(key)
    return tables[0]


def draw_route_slots(key, part):
    tables = route_tables(key)
    return tables[1]


def spiked(values, own_key, source, target, parts, factor):
    owner, partner = [(jnp.arange(values.shape[position]) // (values.shape[position] // parts)).reshape([-1 if axis == position else 1 for axis in range(values.ndim)]) for position in (source, target)]
    chosen = jax.random.permutation(own_key, parts)[partner]
    strong = (owner == chosen) | (owner == (partner + parts // 2) % parts)
    return jnp.where(strong, factor * values, values)


def levels(key, shape, pieces, least, top_value):
    def one(axis_at, parts):
        heights = jax.random.uniform(jax.random.fold_in(jax.random.fold_in(key, 6), axis_at), (parts,), jnp.float32, least / len(pieces), top_value / len(pieces))
        return jnp.repeat(jnp.exp(heights), shape[axis_at] // parts).reshape((-1,) + (1,) * (len(shape) - axis_at - 1))

    gain = one(*pieces[0])
    for cut in pieces[1:]:
        gain = gain * one(*cut)
    return gain


def gaussian(stream_key, extent, deviation, limit, cuts=(), held_as=jnp.bfloat16):
    drawn = deviation * jax.random.normal(stream_key, extent, jnp.float32)
    if cuts:
        drawn = drawn * levels(stream_key, extent, cuts, -0.22, 0.18)
    return jnp.clip(drawn, -limit, limit).astype(held_as)


def bell_draw_with(stream_key, extent, scale, bound, pieces, heavy, held_as=jnp.bfloat16):
    drawn = scale * jax.random.normal(stream_key, extent, jnp.float32)
    if pieces:
        drawn = drawn * levels(stream_key, extent, pieces, -0.22, 0.18)
    return jnp.clip(spiked(drawn, jax.random.fold_in(stream_key, 3), *heavy), -bound, bound).astype(held_as)


def setup_inputs(seed: int = 0) -> dict:
    key_list = jax.random.split(jax.random.key(seed), 16)
    tokens = bell_draw_with(key_list[0], (SEQS, LEN, D), 1.0, 6.0, ((0, 16), (1, 4)), (0, 2, 16, 2.0))
    cotangent = bell_draw_with(key_list[1], (SEQS, LEN, D), 1.0, 6.0, ((0, 16), (1, 4)), (0, 2, 16, 2.0))
    route_experts = draw_route_experts(jax.random.fold_in(key_list[15], 71), 0)
    route_slots = draw_route_slots(jax.random.fold_in(key_list[15], 71), 0)
    gain_attn = jnp.clip(1.0 + 0.1 * jax.random.normal(key_list[4], (LAYERS, D), jnp.float32), 0.5, 1.5).astype(jnp.bfloat16)
    w_query = gaussian(key_list[5], (LAYERS, D, HQ * HD), D ** -0.5, 0.15625, ((0, 2), (1, 16), (2, 4)))
    w_key = gaussian(key_list[6], (LAYERS, D, HK * HD), D ** -0.5, 0.15625, ((0, 2), (1, 16), (2, 4)))
    w_value = gaussian(key_list[7], (LAYERS, D, HK * HD), D ** -0.5, 0.15625, ((0, 2), (1, 16), (2, 4)))
    w_out = gaussian(key_list[8], (LAYERS, HQ * HD, D), (HQ * HD // 16) ** -0.5, 0.625, ((0, 2), (1, 4), (2, 16)))
    gain_ffn = jnp.clip(1.0 + 0.1 * jax.random.normal(key_list[9], (LAYERS, D), jnp.float32), 0.5, 1.5).astype(jnp.bfloat16)
    w_router = gaussian(key_list[10], (LAYERS, D, E), (4 * D) ** -0.5, 0.078125, ((0, 2), (1, 64)))
    w_shared_in = gaussian(key_list[11], (LAYERS, D, 2, FFS), D ** -0.5, 0.15625, ((0, 2), (1, 16), (3, 4)))
    w_shared_down = gaussian(key_list[12], (LAYERS, FFS, D), (FFS // 2) ** -0.5, 0.25, ((0, 2), (1, 4), (2, 16)))
    w_expert_in = gaussian(key_list[13], (LAYERS, D, E, 2, FFE), D ** -0.5, 0.15625, ((0, 2), (1, 16), (4, 4)))
    w_expert_down = gaussian(key_list[14], (LAYERS, E, FFE, D), (FFE // 8) ** -0.5, 0.75, ((0, 2), (2, 4), (3, 16)))
    return {"tokens": tokens, "cotangent": cotangent, "route_experts": route_experts, "route_slots": route_slots, "gain_attn": gain_attn, "w_query": w_query, "w_key": w_key, "w_value": w_value, "w_out": w_out, "gain_ffn": gain_ffn, "w_router": w_router, "w_shared_in": w_shared_in, "w_shared_down": w_shared_down, "w_expert_in": w_expert_in, "w_expert_down": w_expert_down}


@jax.custom_vjp
def low(v):
    return lax.optimization_barrier(v.astype(jnp.bfloat16)).astype(jnp.float32)

@jax.custom_vjp
def low_back(v):
    return v

def low_keep(v):
    return (low(v), None)

def low_pass(kept, grad):
    return (grad,)

def back_keep(v):
    return (v, None)

def back_low(kept, grad):
    return (low(grad),)
low.defvjp(low_keep, low_pass)
low_back.defvjp(back_keep, back_low)
NORM_EPSILON = 1e-05
MASK_VALUE = -1e+30
EXACT = lax.Precision.HIGHEST

def normalize(rows_in, gain_vec):
    return rows_in * lax.rsqrt(lax.optimization_barrier(jnp.mean(rows_in * rows_in, axis=-1, keepdims=True)) + NORM_EPSILON) * gain_vec

def softmax_last(values):
    shifted = jnp.exp(values - lax.optimization_barrier(jnp.max(values, axis=-1, keepdims=True)))
    return shifted / lax.optimization_barrier(jnp.sum(shifted, axis=-1, keepdims=True))

def layer_sequence(hidden_in, weights, experts, slot_ids):
    gain_attn, w_query, w_key, w_value, w_out, gain_ffn, w_router, w_shared_in, w_shared_down, w_expert_in, w_expert_down = weights
    length = hidden_in.shape[0]
    groups = HQ // HK
    normed = low(normalize(hidden_in, gain_attn))
    queries = low_back(low(jnp.dot(normed, w_query, precision=EXACT))).reshape(length, HK, groups, HD)
    keys_all = low_back(low(jnp.dot(normed, w_key, precision=EXACT))).reshape(length, HK, HD)
    values_all = low_back(low(jnp.dot(normed, w_value, precision=EXACT))).reshape(length, HK, HD)
    raw_scores = jnp.einsum('qgid,kgd->giqk', queries, keys_all, precision=EXACT)
    scores = low_back(raw_scores) * HD ** (-0.5)
    positions = jnp.arange(length)
    causal = positions[None, :] <= positions[:, None]
    attn_probs = softmax_last(jnp.where(causal, scores, MASK_VALUE))
    attended = jnp.einsum('giqk,kgd->qgid', low(attn_probs), values_all, precision=EXACT)
    attended = low_back(low(attended)).reshape(length, HQ * HD)
    mid_rows = hidden_in + low_back(jnp.dot(attended, w_out, precision=EXACT))
    normed_ffn = low(normalize(mid_rows, gain_ffn))
    logits = low_back(jnp.dot(normed_ffn, w_router, precision=EXACT))
    gate_weights = softmax_last(jnp.take_along_axis(logits, experts, axis=1))
    flat_slots = (experts * CAP + slot_ids).reshape(-1)
    dispatched = jnp.zeros((E * CAP, normed_ffn.shape[1]), normed_ffn.dtype)
    dispatched = dispatched.at[flat_slots].set(jnp.repeat(normed_ffn, TOPK, axis=0)).reshape(E, CAP, -1)
    gate_up = low_back(jnp.einsum('ecd,dekf->eckf', dispatched, w_expert_in, precision=EXACT))
    expert_hidden = low(jax.nn.silu(gate_up[:, :, 0]) * gate_up[:, :, 1])
    expert_rows = low_back(jnp.einsum('ecf,efd->ecd', expert_hidden, w_expert_down, precision=EXACT))
    picked = expert_rows.reshape(E * CAP, -1)[flat_slots].reshape(length, TOPK, -1)
    routed = jnp.einsum('tj,tjd->td', gate_weights, picked, precision=EXACT)
    shared_in = low_back(jnp.einsum('td,dkf->tkf', normed_ffn, w_shared_in, precision=EXACT))
    shared_hidden = low(jax.nn.silu(shared_in[:, 0]) * shared_in[:, 1])
    shared_out = jnp.dot(shared_hidden, w_shared_down, precision=EXACT)
    return low_back(low(mid_rows + low_back(routed + shared_out)))

def forward(tokens_in, probes, params, route_experts, route_slots):
    current = tokens_in
    layer_values = []
    batched = jax.checkpoint(jax.vmap(layer_sequence, in_axes=(0, None, 0, 0)))
    for layer_index in range(LAYERS):
        weights = tuple((weight_set[layer_index] for weight_set in params))
        grouped = ((current + probes[layer_index]).reshape(SEQS // MICRO, MICRO, LEN, D), route_experts[layer_index].reshape(SEQS // MICRO, MICRO, LEN, TOPK), route_slots[layer_index].reshape(SEQS // MICRO, MICRO, LEN, TOPK))
        current = lax.map(lambda group_args: batched(group_args[0], weights, group_args[1], group_args[2]), grouped)
        current = current.reshape(SEQS, LEN, D)
        layer_values.append(current)
    return (current, jnp.stack(layer_values))

def reference(tokens, cotangent, route_experts, route_slots, gain_attn, w_query, w_key, w_value, w_out, gain_ffn, w_router, w_shared_in, w_shared_down, w_expert_in, w_expert_down):
    params = tuple((weight_set.astype(jnp.float32) for weight_set in (gain_attn, w_query, w_key, w_value, w_out, gain_ffn, w_router, w_shared_in, w_shared_down, w_expert_in, w_expert_down)))
    tokens_in = tokens.astype(jnp.float32)
    probes = jnp.zeros((LAYERS,) + tokens.shape, jnp.float32)

    def run(probe_values, *weight_values):
        return forward(tokens_in, probe_values, weight_values, route_experts, route_slots)
    final_rows, pullback, layer_values = jax.vjp(run, probes, *params, has_aux=True)
    grad_set = pullback(cotangent.astype(jnp.float32))
    return (layer_values.astype(jnp.bfloat16), grad_set[0].astype(jnp.bfloat16), grad_set[1], grad_set[2], grad_set[3], grad_set[4], grad_set[5], grad_set[6], grad_set[7], grad_set[8], grad_set[9], grad_set[10], grad_set[11])
```

```python
import jax
import jax.numpy as jnp
from jax import lax
from jax.sharding import Mesh
from jax.sharding import PartitionSpec as P

D = 1536
HD = 128
E = 16
HALF_E = 8
GROUPS = 3
LEN = 256
ROWS = 64
DBLK = 96
HALF = D // 2

NORM_EPSILON = 1e-05
MASK_VALUE = -1e30
SCALE = HD**-0.5

BF = jnp.bfloat16
F32 = jnp.float32

QKV = 640
ATT = 1024
ATT_PAD = 1152
BLOCKS = 9
UP = BLOCKS * 256
DOWN = BLOCKS * 128

SECTION = ("section",)
TENSOR = ("tensor",)
GROUP = ("section", "tensor")
CORE = ("core",)
ROW = ("z",)
SIDE = ("section", "xhi")


def dot(a, b, contract):
    return lax.dot_general(a, b, ((contract[:1], contract[1:]), ((), ())), preferred_element_type=F32)


def nn(a, b):
    return dot(a, b, (1, 0))


def nt(a, b):
    return dot(a, b, (1, 1))


def tn(a, b):
    return dot(a, b, (0, 0))


def move(block, axes, target, only=None):
    sizes = [lax.axis_size(axis) for axis in axes]
    pairs = []

    def flat(place):
        index = 0
        for size, at in zip(sizes, place):
            index = index * size + at % size
        return index

    def walk(place):
        if len(place) == len(sizes):
            if only is None or only(*place):
                pairs.append((flat(place), flat(target(*place))))
            return
        for at in range(sizes[len(place)]):
            walk(place + (at,))

    walk(())
    return lax.ppermute(block, axes, pairs)


def tensor_gather(rows):
    return [rows] + [move(rows, TENSOR, lambda t, k=k: (t - k,)) for k in (1, 2, 3)]


def tensor_sum(parts):
    parts = parts.reshape(4, ROWS, -1)
    low = parts.astype(BF)
    total = parts[0].astype(F32)
    for k in (1, 2, 3):
        total = total + move(low[k], TENSOR, lambda t, k=k: (t + k,)).astype(F32)
    return total


def group_gather(rows):
    blocks = []
    for a in (0, 1):
        for k in range(4):
            if a or k:
                blocks.append(move(rows, GROUP, lambda s, t, a=a, k=k: (s - a, t - k)))
            else:
                blocks.append(rows)
    return jnp.concatenate(blocks, axis=0)


def group_sum(parts):
    parts = parts.reshape(8, ROWS, -1)
    low = parts.astype(BF)
    total = parts[0].astype(F32)
    for a in (1, 0):
        for k in range(4):
            if a or k:
                got = move(low[4 * a + k], GROUP, lambda s, t, a=a, k=k: (s + a, t + k))
                total = total + got.astype(F32)
    return total


def rolled(stacked, shift):
    n = stacked.shape[0]
    return lax.dynamic_slice_in_dim(jnp.concatenate([stacked, stacked], axis=0), shift, n, 0)


def rms_factor(rows):
    return lax.rsqrt(jnp.mean(rows * rows, axis=-1, keepdims=True) + NORM_EPSILON)


def norm_backward(rows, factor, gain, upstream):
    unit = rows * factor
    scaled = upstream * gain
    grad = factor * (scaled - unit * jnp.mean(scaled * unit, axis=-1, keepdims=True))
    return grad, jnp.sum(upstream * unit, axis=0)


def by_halves(fn, rows, halves):
    return fn(rows[:, :HALF], halves[0]) + fn(rows[:, HALF:], halves[1])


def to_halves(rows, halves):
    return jnp.concatenate([nt(rows, halves[0]), nt(rows, halves[1])], axis=1)


def swap_core(block):
    return (block, move(block, CORE, lambda c: (1 - c,)))


def attention_forward(hidden_rows, weights, gain, causal):
    hidden = hidden_rows.astype(F32)
    factor = rms_factor(hidden)
    normed = (hidden * factor * gain).astype(BF)
    qkv = by_halves(nn, normed, [w[:, :QKV] for w in weights]).astype(BF)
    queries = qkv[:, : GROUPS * HD].reshape(LEN, GROUPS, HD)
    keys = qkv[:, GROUPS * HD : GROUPS * HD + HD]
    values = qkv[:, GROUPS * HD + HD :]
    scores = jnp.einsum("qgd,kd->gqk", queries, keys, preferred_element_type=F32) * SCALE
    scores = jnp.where(causal[None], scores, MASK_VALUE)
    shifted = jnp.exp(scores - jnp.max(scores, axis=-1, keepdims=True))
    probs = shifted / jnp.sum(shifted, axis=-1, keepdims=True)
    attended = jnp.einsum("gqk,kd->qgd", probs.astype(BF), values, preferred_element_type=F32)
    attended = attended.astype(BF).reshape(LEN, GROUPS * HD)
    part = to_halves(attended, [w[:, QKV:ATT] for w in weights])
    return part, (normed, queries, keys, values, probs, attended)


def attention_backward(grad_rows, weights, saved):
    normed, queries, keys, values, probs, attended = saved
    attended_grad = by_halves(nn, grad_rows, [w[:, QKV:ATT] for w in weights]).astype(BF)
    attended_grad = attended_grad.reshape(LEN, GROUPS, HD)
    value_grad = jnp.einsum("gqk,qgd->kd", probs.astype(BF), attended_grad, preferred_element_type=F32)
    prob_grad = jnp.einsum("qgd,kd->gqk", attended_grad, values, preferred_element_type=F32)
    score_grad = probs * (prob_grad - jnp.sum(probs * prob_grad, axis=-1, keepdims=True))
    score_grad = (score_grad * SCALE).astype(BF)
    query_grad = jnp.einsum("gqk,kd->qgd", score_grad, keys, preferred_element_type=F32)
    key_grad = jnp.einsum("gqk,qgd->kd", score_grad, queries, preferred_element_type=F32)
    qkv_grad = jnp.concatenate(
        [query_grad.reshape(LEN, GROUPS * HD), key_grad, value_grad], axis=1
    ).astype(BF)
    part = to_halves(qkv_grad, [w[:, :QKV] for w in weights])
    return part, qkv_grad


def masked_softmax(logits, mask):
    top = jnp.max(jnp.where(mask, logits, MASK_VALUE), axis=-1, keepdims=True)
    shifted = jnp.where(mask, jnp.exp(jnp.where(mask, logits - top, 0.0)), 0.0)
    return shifted / jnp.sum(shifted, axis=-1, keepdims=True)


def spread(gates):
    return jnp.concatenate([gates, jnp.ones((gates.shape[0], 1), F32)], axis=1)[:, :, None]


def ffn_forward(rows, weights, gates):
    gate_up = by_halves(nn, rows, [w[:, :UP] for w in weights])
    parts = gate_up.reshape(-1, BLOCKS, 2, HD)
    hidden = jax.nn.silu(parts[:, :, 0]) * parts[:, :, 1]
    gated = (hidden * spread(gates)).astype(BF).reshape(-1, DOWN)
    out = to_halves(gated, [w[:, UP:] for w in weights])
    return out, (gate_up, gated)


def ffn_backward(grad_rows, weights, saved, gates):
    gate_up, gated = saved
    hidden_grad = by_halves(nn, grad_rows, [w[:, UP:] for w in weights]).reshape(-1, BLOCKS, HD)
    parts = gate_up.reshape(-1, BLOCKS, 2, HD)
    gate_part, up_part = parts[:, :, 0], parts[:, :, 1]
    sigmoid = jax.nn.sigmoid(gate_part)
    silu = gate_part * sigmoid
    products = jnp.sum((silu * up_part * hidden_grad)[:, :HALF_E], axis=-1)
    hidden_grad = hidden_grad * spread(gates)
    gate_grad = hidden_grad * up_part * sigmoid * (1.0 + gate_part * (1.0 - sigmoid))
    up_grad = hidden_grad * silu
    gate_up_grad = jnp.stack([gate_grad, up_grad], axis=2).astype(BF).reshape(-1, UP)
    part = to_halves(gate_up_grad, [w[:, :UP] for w in weights])
    return part, products, gate_up_grad


def weight_halves(lefts, rights):
    halves = []
    for at in (0, 1):
        cut = slice(at * HALF, (at + 1) * HALF)
        halves.append(
            jnp.concatenate([tn(left[:, cut], right) for left, right in zip(lefts, rights)], axis=1)
        )
    return halves


def reduce_rows(halves):
    other = move(halves[1].astype(BF), CORE, lambda c: (1 - c,))
    own = (halves[0] + other.astype(F32)).astype(BF)
    return lax.psum_scatter(own, "z", scatter_dimension=0, tiled=True).reshape(2, DBLK, -1)


def send_home(blocks, home):
    beside = move(blocks[1], SIDE, lambda s, x: (s, x + 1), lambda s, x: s == home)
    straight = move(blocks[0], SIDE, lambda s, x: (s + 1, x), lambda s, x: s != home)
    across = move(blocks[1], SIDE, lambda s, x: (s + 1, x + 1), lambda s, x: s != home)
    own = blocks[0].astype(F32) + beside.astype(F32)
    return own, straight.astype(F32) + across.astype(F32)


def per_device(
    tokens,
    cotangent,
    route_experts,
    route_slots,
    gain_attn,
    w_query,
    w_key,
    w_value,
    w_out,
    gain_ffn,
    w_router,
    w_shared_in,
    w_shared_down,
    w_expert_in,
    w_expert_down,
):
    s = lax.axis_index("section")
    xhi = lax.axis_index("xhi")
    core = lax.axis_index("core")
    z = lax.axis_index("z")
    t = lax.axis_index("tensor")
    first = s == 0

    own_tokens = lax.dynamic_index_in_dim(tokens, s, 0, keepdims=False)
    own_cotangent = lax.dynamic_index_in_dim(cotangent, s, 0, keepdims=False)
    token_blocks = tensor_gather(own_tokens)

    small = jnp.concatenate(
        [gain_attn[0][:, None], gain_ffn[0][:, None], w_router[0], jnp.zeros((24, 110), BF)], axis=1
    )
    small = lax.all_gather(small, "tensor", axis=0, tiled=True)
    att_piece = jnp.concatenate([w_query[0], w_key[0], w_value[0], w_out[0].T, small], axis=1)

    expert_in = w_expert_in[0].reshape(DBLK, 2, HALF_E * 256)
    shared_in = w_shared_in[0].reshape(DBLK, 2, 2, HD)
    expert_down = w_expert_down[0].transpose(2, 0, 1).reshape(DBLK, 2, HALF_E * HD)
    shared_down = w_shared_down[0].T.reshape(DBLK, 2, HD)

    def ffn_piece(part):
        return jnp.concatenate(
            [
                expert_in[:, part],
                shared_in[:, :, part].reshape(DBLK, 2 * HD),
                expert_down[:, part],
                shared_down[:, part],
            ],
            axis=1,
        )

    ffn_own = jnp.where(first, ffn_piece(0), ffn_piece(1))
    ffn_other = jnp.where(first, ffn_piece(1), ffn_piece(0))

    att_beside = move(att_piece, SIDE, lambda s, x: (s, x + 1))
    att_straight = move(att_piece, SIDE, lambda s, x: (s + 1, x))
    att_across = move(att_piece, SIDE, lambda s, x: (s + 1, x + 1))
    att_same = jnp.concatenate([att_piece, att_beside], axis=0)
    att_else = jnp.concatenate([att_straight, att_across], axis=0)
    att_pairs = [jnp.where(first, att_same, att_else), jnp.where(first, att_else, att_same)]

    ffn_straight = move(ffn_other, SIDE, lambda s, x: (s + 1, x))
    ffn_across = move(ffn_other, SIDE, lambda s, x: (s + 1, x + 1))
    ffn_beside0 = move(ffn_own, SIDE, lambda s, x: (s, x + 1), lambda s, x: s == 0)
    ffn_else = jnp.concatenate([ffn_straight, ffn_across], axis=0)
    ffn_pair0 = jnp.where(first, jnp.concatenate([ffn_own, ffn_beside0], axis=0), ffn_else)
    ffn_beside1 = move(ffn_own, SIDE, lambda s, x: (s, x + 1), lambda s, x: s == 1)
    ffn_pair1 = jnp.where(first, ffn_else, jnp.concatenate([ffn_own, ffn_beside1], axis=0))

    att_z = [att_pairs[0]] + [move(att_pairs[0], ROW, lambda at, k=k: (at - k,)) for k in (1, 2, 3)]
    att_rows = rolled(jnp.stack(att_z), (4 - z) % 4).reshape(HALF, ATT_PAD)
    att_w = [swap_core(att_rows)]
    ffn_w = [swap_core(lax.all_gather(ffn_pair0, "z", axis=0, tiled=True))]
    att_w.append(swap_core(lax.all_gather(att_pairs[1], "z", axis=0, tiled=True)))
    ffn_w.append(swap_core(lax.all_gather(ffn_pair1, "z", axis=0, tiled=True)))

    place = jnp.arange(D, dtype=jnp.int32)
    at_core = (place // HALF + core) % 2
    at_z = (place // (2 * DBLK)) % 4
    at_x = (place // DBLK + xhi) % 2
    column = at_x * HALF + at_z * (2 * DBLK) + at_core * DBLK + place % DBLK
    order = (place[:, None] == column[None, :]).astype(BF)

    def reorder(rows):
        return nn(rows, order).astype(BF)

    def restore(rows):
        return nt(rows, order).astype(BF)

    position = (t * ROWS + jnp.arange(LEN, dtype=jnp.int32)) % LEN
    causal = position[None, :] <= position[:, None]

    named = jnp.sum((route_experts[0][:, :, :, None] == jnp.arange(E)).astype(F32), axis=2)
    named = named.astype(BF).reshape(2 * LEN, E)
    named_else = move(named, SECTION, lambda s: (s + 1,))

    def layer_mask(layer):
        mask = jnp.where(s == layer, named, named_else).reshape(2, 4, ROWS, E)
        mask = rolled(rolled(mask, s).swapaxes(0, 1), t).swapaxes(0, 1)
        return mask.reshape(2 * LEN, E) > 0.5

    masks = [layer_mask(0), layer_mask(1)]

    def small_of(layer):
        low = jnp.concatenate([w[:, ATT:] for w in att_w[layer]], axis=0)
        return low[:, 0].astype(F32), low[:, 1].astype(F32), low[:, 2 : 2 + E]

    hidden_blocks = reorder(jnp.concatenate(token_blocks, axis=0))
    own_hidden = hidden_blocks[:ROWS]
    layer_values = []
    kept = []
    for layer in (0, 1):
        attn_gain, ffn_gain, router = small_of(layer)
        hidden = own_hidden.astype(F32)
        part, att_saved = attention_forward(hidden_blocks, att_w[layer], attn_gain, causal)
        mid = hidden + tensor_sum(part)
        factor_ffn = rms_factor(mid)
        normed_ffn = (mid * factor_ffn * ffn_gain).astype(BF)
        rows = group_gather(normed_ffn)
        gates = masked_softmax(nn(rows, router), masks[layer])
        own_gates = lax.dynamic_slice_in_dim(gates, s * HALF_E, HALF_E, 1)
        out, ffn_saved = ffn_forward(rows, ffn_w[layer], own_gates)
        result = (mid + group_sum(out)).astype(BF)
        layer_values.append(result)
        kept.append((hidden, mid, factor_ffn, rows, gates, own_gates, att_saved, ffn_saved))
        own_hidden = result
        if layer == 0:
            hidden_blocks = jnp.concatenate(tensor_gather(result), axis=0)

    out_low = reorder(own_cotangent)
    in_grads = [None, None]
    small_grads = [None, None]
    att_sums = [None, None]
    ffn_sums = [None, None]
    for layer in (1, 0):
        attn_gain, ffn_gain, router = small_of(layer)
        hidden, mid, factor_ffn, rows, gates, own_gates, att_saved, ffn_saved = kept[layer]
        out_grad = out_low.astype(F32)
        grad_rows = group_gather(out_low)
        part, products, gate_up_grad = ffn_backward(grad_rows, ffn_w[layer], ffn_saved, own_gates)
        empty = jnp.zeros_like(products)
        products = jnp.where(
            first,
            jnp.concatenate([products, empty], axis=1),
            jnp.concatenate([empty, products], axis=1),
        )
        high = products.astype(BF)
        rest = (products - high.astype(F32)).astype(BF)
        extra = jnp.concatenate([high, rest, jnp.zeros((2 * LEN, HD - 2 * E), BF)], axis=1)
        summed = group_sum(jnp.concatenate([part.astype(BF), extra], axis=1))
        ffn_sums[layer] = reduce_rows(weight_halves([rows, grad_rows], [gate_up_grad, ffn_saved[1]]))
        gate_grad = summed[:, D : D + E] + summed[:, D + E : D + 2 * E]
        own = gates[:ROWS]
        logits_grad = own * (gate_grad - jnp.sum(own * gate_grad, axis=1, keepdims=True))
        logits_grad = logits_grad.astype(BF)
        ffn_in_grad = summed[:, :D] + nt(logits_grad, router)
        mid_norm_grad, grad_gain_ffn = norm_backward(mid, factor_ffn, ffn_gain, ffn_in_grad)
        mid_grad = out_grad + mid_norm_grad
        mid_rows = jnp.concatenate(tensor_gather(mid_grad.astype(BF)), axis=0)
        part, qkv_grad = attention_backward(mid_rows, att_w[layer], att_saved)
        normed_grad = tensor_sum(part)
        att_sums[layer] = reduce_rows(
            weight_halves([att_saved[0], mid_rows], [qkv_grad, att_saved[5]])
        )
        hidden_norm_grad, grad_gain_attn = norm_backward(
            hidden, rms_factor(hidden), attn_gain, normed_grad
        )
        out_low = (mid_grad + hidden_norm_grad).astype(BF)
        in_grads[layer] = out_low
        grad_router = tn(rows[:ROWS], logits_grad)
        small_grads[layer] = jnp.concatenate(
            [grad_gain_attn[:, None], grad_gain_ffn[:, None], grad_router], axis=1
        )

    def both_sequences(values):
        low = restore(jnp.concatenate(values, axis=0)).reshape(2, ROWS, D)
        mine = jnp.where(first, low[0], low[1])
        got = move(jnp.where(first, low[1], low[0]), SECTION, lambda s: (s + 1,))
        return jnp.where(first, jnp.stack([mine, got]), jnp.stack([got, mine]))[None]

    values_out = both_sequences(layer_values)
    grads_in = both_sequences(in_grads)

    att_home = [send_home(att_sums[layer], layer) for layer in (0, 1)]
    ffn_home = [send_home(ffn_sums[layer], layer) for layer in (0, 1)]
    att = jnp.where(first, att_home[0][0] + att_home[0][1], att_home[1][0] + att_home[1][1])
    ffn_mine = jnp.where(first, ffn_home[0][0], ffn_home[1][0])
    ffn_got = jnp.where(first, ffn_home[0][1], ffn_home[1][1])
    low_part = jnp.where(first, ffn_mine, ffn_got)
    high_part = jnp.where(first, ffn_got, ffn_mine)

    def reduce_small(values):
        values = values.reshape(2, 4, 2, DBLK, 2, 2 + E)
        values = values[0] + move(values[1], CORE, lambda c: (1 - c,))
        values = rolled(values, z)
        total = values[0]
        for k in (1, 2, 3):
            total = total + move(values[k], ROW, lambda at, k=k: (at + k,))
        total = total[0] + move(total[1], ("xhi",), lambda x: (x + 1,))
        mine = jnp.where(first, total[:, 0], total[:, 1])
        total = mine + move(jnp.where(first, total[:, 1], total[:, 0]), SECTION, lambda s: (s + 1,))
        total = lax.psum(total, "tensor")
        return lax.dynamic_slice_in_dim(total, t * 24, 24, 0)

    small_sum = reduce_small(jnp.stack(small_grads, axis=1))

    def blocks_of(at, count):
        return [part[:, at : at + count] for part in (low_part, high_part)]

    grad_expert_in = jnp.stack(blocks_of(0, HALF_E * 256), axis=1).reshape(DBLK, E, 2, HD)
    grad_shared_in = jnp.concatenate(
        [part.reshape(DBLK, 2, HD) for part in blocks_of(HALF_E * 256, 256)], axis=2
    )
    grad_expert_down = jnp.concatenate(blocks_of(UP, HALF_E * HD), axis=1)
    grad_expert_down = grad_expert_down.reshape(DBLK, E, HD).transpose(1, 2, 0)
    grad_shared_down = jnp.concatenate(blocks_of(UP + HALF_E * HD, HD), axis=1).T
    return (
        values_out,
        grads_in,
        small_sum[:, 0][None],
        att[:, : GROUPS * HD][None],
        att[:, GROUPS * HD : GROUPS * HD + HD][None],
        att[:, GROUPS * HD + HD : QKV][None],
        att[:, QKV:].T[None],
        small_sum[:, 1][None],
        small_sum[:, 2:][None],
        grad_shared_in[None],
        grad_shared_down[None],
        grad_expert_in[None],
        grad_expert_down[None],
    )


def solution(mesh):
    split = Mesh(
        mesh.devices.reshape(2, 2, 4, 2, 4), ("section", "xhi", "z", "core", "tensor")
    )
    dp = ("xhi", "z", "core")
    both = dp + ("tensor",)
    placed = (
        P(dp, "tensor", None),
        P(dp, "tensor", None),
        P("section", dp, None, None),
        P("section", dp, None, None),
        P("section", both),
        P("section", dp, "tensor"),
        P("section", dp, "tensor"),
        P("section", dp, "tensor"),
        P("section", "tensor", dp),
        P("section", both),
        P("section", both, None),
        P("section", dp, None, "tensor"),
        P("section", "tensor", dp),
        P("section", dp, None, None, "tensor"),
        P("section", None, "tensor", dp),
    )
    return jax.shard_map(
        per_device,
        mesh=split,
        in_specs=placed,
        out_specs=(
            P("section", dp, "tensor", None),
            P("section", dp, "tensor", None),
            P("section", both),
            P("section", dp, "tensor"),
            P("section", dp, "tensor"),
            P("section", dp, "tensor"),
            P("section", "tensor", dp),
            P("section", both),
            P("section", both, None),
            P("section", dp, None, "tensor"),
            P("section", "tensor", dp),
            P("section", dp, None, None, "tensor"),
            P("section", None, "tensor", dp),
        ),
        check_vma=False,
    )
```

```python
import jax
import jax.numpy as jnp
from jax import lax
from jax.experimental import pallas as pl
from jax.experimental.pallas import tpu as pltpu
from jax.sharding import Mesh
from jax.sharding import PartitionSpec as P

D = 1536
HD = 128
E = 16
HALF_E = 8
GROUPS = 3
LEN = 256
ROWS = 64
DBLK = 96
HALF = D // 2
ROUTES = 2 * LEN

NORM_EPSILON = 1e-05
MASK_VALUE = -1e30
SCALE = HD**-0.5

BF = jnp.bfloat16
F32 = jnp.float32

QKV = 640
ATT = 1024
ATT_PAD = 1152
BLOCKS = 9
STEPS = 3
STEP = 3 * HD
UP = BLOCKS * 256
DOWN = BLOCKS * 128
PIECE = UP + DOWN
WIDE = D + HD
SMALL = 24

SECTION = ("section",)
TENSOR = ("tensor",)
GROUP = ("section", "tensor")
CORE = ("core",)
ROW = ("z",)
SIDE = ("section", "xhi")


def dot(a, b, contract):
    return lax.dot_general(a, b, ((contract[:1], contract[1:]), ((), ())), preferred_element_type=F32)


def nn(a, b):
    return dot(a, b, (1, 0))


def nt(a, b):
    return dot(a, b, (1, 1))


def tn(a, b):
    return dot(a, b, (0, 0))


def move(block, axes, target, only=None):
    sizes = [lax.axis_size(axis) for axis in axes]
    pairs = []

    def flat(place):
        index = 0
        for size, at in zip(sizes, place):
            index = index * size + at % size
        return index

    def walk(place):
        if len(place) == len(sizes):
            if only is None or only(*place):
                pairs.append((flat(place), flat(target(*place))))
            return
        for at in range(sizes[len(place)]):
            walk(place + (at,))

    walk(())
    return lax.ppermute(block, axes, pairs)

VMEM = pl.BlockSpec(memory_space=pltpu.VMEM)
SMEM = pl.BlockSpec(memory_space=pltpu.SMEM)


def shaped(shape, dtype=BF):
    return jax.ShapeDtypeStruct(shape, dtype)


def run(kernel, outs, operands, scalars=0, flops=0, in_specs=None, out_specs=None, grid=(), scratch=()):
    if in_specs is None:
        in_specs = [SMEM] * scalars + [VMEM] * (len(operands) - scalars)
    if out_specs is None:
        out_specs = [VMEM] * len(outs)
    moved = sum(x.size * x.dtype.itemsize for x in list(operands) + list(outs))
    return pl.pallas_call(
        kernel,
        out_shape=list(outs),
        in_specs=in_specs,
        out_specs=out_specs,
        grid=grid,
        scratch_shapes=list(scratch),
        compiler_params=pltpu.CompilerParams(vmem_limit_bytes=48 * 1024 * 1024),
        cost_estimate=pl.CostEstimate(flops=flops, bytes_accessed=moved, transcendentals=0),
    )(*operands)


def together(*values):
    return lax.optimization_barrier(values)


def tensor_gather(rows):
    return [rows] + [move(rows, TENSOR, lambda t, k=k: (t - k,)) for k in (1, 2, 3)]


def tensor_send(parts):
    return [move(parts[k], TENSOR, lambda t, k=k: (t + k,)) for k in (1, 2, 3)]


def group_exchange(rows):
    return lax.all_to_all(rows, GROUP, 0, 0, tiled=True)


def rolled(stacked, shift):
    n = stacked.shape[0]
    return lax.dynamic_slice_in_dim(jnp.concatenate([stacked, stacked], axis=0), shift, n, 0)


def rms_factor(rows):
    return lax.rsqrt(jnp.mean(rows * rows, axis=-1, keepdims=True) + NORM_EPSILON)


def norm_backward(rows, gain, upstream):
    factor = rms_factor(rows)
    unit = rows * factor
    scaled = upstream * gain
    grad = factor * (scaled - unit * jnp.mean(scaled * unit, axis=-1, keepdims=True))
    return grad, jnp.sum(upstream * unit, axis=0, keepdims=True)


def add_up(refs):
    total = refs[0][...].astype(F32)
    for ref in refs[1:]:
        total = total + ref[...].astype(F32)
    return total


def block(index):
    return slice(index * ROWS, (index + 1) * ROWS)


def add_blocks(ref):
    total = ref[block(0), :].astype(F32)
    for index in range(1, 8):
        total = total + ref[block(index), :].astype(F32)
    return total


def head(index):
    return slice(index * HD, (index + 1) * HD)


KEYS = head(GROUPS)
VALUES = head(GROUPS + 1)


def attention_forward_kernel(t_ref, *refs):
    hidden, (w0, w1) = refs[:4], refs[4:6]
    parts, (normed_ref, qkv_ref, probs_ref, attended_ref, small_ref) = refs[6:10], refs[10:]
    for at, w in ((0, w0), (HALF, w1)):
        small_ref[:, at : at + HALF] = w[:, ATT:].astype(F32).T[:SMALL]
    for index, ref in enumerate(hidden):
        rows = ref[...].astype(F32)
        normed_ref[block(index), :] = (rows * rms_factor(rows) * small_ref[0:1, :]).astype(BF)
    normed = normed_ref[...]
    qkv = nn(normed[:, :HALF], w0[:, :QKV]) + nn(normed[:, HALF:], w1[:, :QKV])
    qkv = qkv.astype(BF)
    qkv_ref[...] = qkv

    def position(axis):
        return (t_ref[0] * ROWS + lax.broadcasted_iota(jnp.int32, (LEN, LEN), axis)) & (LEN - 1)

    causal = position(1) <= position(0)
    for g in range(GROUPS):
        scores = jnp.where(causal, nt(qkv[:, head(g)], qkv[:, KEYS]) * SCALE, MASK_VALUE)
        shifted = jnp.exp(scores - jnp.max(scores, axis=-1, keepdims=True))
        probs = (shifted / jnp.sum(shifted, axis=-1, keepdims=True)).astype(BF)
        probs_ref[g] = probs
        attended_ref[:, head(g)] = nn(probs, qkv[:, VALUES]).astype(BF)
    attended = attended_ref[...]
    for at, w in ((0, w0), (HALF, w1)):
        out = nt(attended, w[:, QKV:ATT]).astype(BF)
        for index, part in enumerate(parts):
            part[:, at : at + HALF] = out[block(index)]


def attention_forward(t, hidden_blocks, weights):
    outs = [shaped((ROWS, D))] * 4
    outs += [shaped((LEN, D)), shaped((LEN, QKV)), shaped((GROUPS, LEN, LEN)), shaped((LEN, STEP))]
    outs += [shaped((SMALL, D), F32)]
    flops = 2 * LEN * D * ATT + 4 * GROUPS * LEN * LEN * HD
    got = run(attention_forward_kernel, outs, [t, *hidden_blocks, *weights], 1, flops)
    return got[:4], got[4:]


def attention_backward_kernel(*refs):
    grads, (w0, w1, qkv_ref, probs_ref) = refs[:4], refs[4:8]
    parts, (rows_ref, qkv_grad_ref) = refs[8:12], refs[12:]
    for index, ref in enumerate(grads):
        rows_ref[block(index), :] = ref[...]
    rows = rows_ref[...]
    attended_grad = nn(rows[:, :HALF], w0[:, QKV:ATT]) + nn(rows[:, HALF:], w1[:, QKV:ATT])
    attended_grad = attended_grad.astype(BF)
    qkv = qkv_ref[...]
    key_grad = jnp.zeros((LEN, HD), F32)
    value_grad = jnp.zeros((LEN, HD), F32)
    for g in range(GROUPS):
        probs = probs_ref[g]
        upstream = attended_grad[:, head(g)]
        value_grad = value_grad + tn(probs, upstream)
        prob_grad = nt(upstream, qkv[:, VALUES])
        wide = probs.astype(F32)
        score_grad = wide * (prob_grad - jnp.sum(wide * prob_grad, axis=-1, keepdims=True))
        score_grad = (score_grad * SCALE).astype(BF)
        qkv_grad_ref[:, head(g)] = nn(score_grad, qkv[:, KEYS]).astype(BF)
        key_grad = key_grad + tn(score_grad, qkv[:, head(g)])
    qkv_grad_ref[:, KEYS] = key_grad.astype(BF)
    qkv_grad_ref[:, VALUES] = value_grad.astype(BF)
    qkv_grad = qkv_grad_ref[...]
    for at, w in ((0, w0), (HALF, w1)):
        out = nt(qkv_grad, w[:, :QKV]).astype(BF)
        for index, part in enumerate(parts):
            part[:, at : at + HALF] = out[block(index)]


def attention_backward(grad_blocks, weights, qkv, probs):
    outs = [shaped((ROWS, D))] * 4 + [shaped((LEN, D)), shaped((LEN, QKV))]
    flops = 2 * LEN * D * ATT + 10 * GROUPS * LEN * LEN * HD
    got = run(attention_backward_kernel, outs, [*grad_blocks, *weights, qkv, probs], 0, flops)
    return got[:4], got[4], got[5]


def attention_weights_kernel(normed, rows, qkv_grad, attended, *refs):
    out = refs[-1]
    for columns, left, right in (
        (slice(0, QKV), normed, qkv_grad),
        (slice(QKV, ATT), rows, attended),
    ):
        total = tn(left[...], right[...])
        if len(refs) > 1:
            total = total + refs[0][:, columns].astype(F32)
        out[:, columns] = total.astype(BF)


def attention_weights(half, normed, rows, qkv_grad, attended, *other):
    def full(*shape):
        return pl.BlockSpec(shape, lambda i: (0, 0))

    cut = pl.BlockSpec((LEN, HALF), lambda i: (0, half))
    in_specs = [cut, cut, full(LEN, QKV), full(LEN, STEP)] + [full(HALF, ATT)] * len(other)
    return run(
        attention_weights_kernel,
        [shaped((HALF, ATT))],
        [normed, rows, qkv_grad, attended, *other],
        flops=2 * HALF * LEN * ATT,
        in_specs=in_specs,
        out_specs=[full(HALF, ATT)],
        grid=(1,),
    )[0]


def gate_column(gates, section, number):
    lane = lax.broadcasted_iota(jnp.int32, gates.shape, 1)
    picked = jnp.where(lane == section * HALF_E + number, gates, 0.0)
    return jnp.where(number == HALF_E, 1.0, jnp.sum(picked, axis=1, keepdims=True))


def ffn_forward_kernel(s_ref, t_ref, rows_ref, router, mask_ref, up0, up1, down0, down1, *refs):
    step = pl.program_id(0)
    part, gates_ref, own_ref, gate_up_ref, gated_ref, total = refs

    @pl.when(step == 0)
    def _():
        logits = nt(rows_ref[...], router[...])
        named = mask_ref[...] > 0.5
        top = jnp.max(jnp.where(named, logits, MASK_VALUE), axis=-1, keepdims=True)
        shifted = jnp.where(named, jnp.exp(jnp.where(named, logits - top, 0.0)), 0.0)
        gates_ref[...] = shifted / jnp.sum(shifted, axis=-1, keepdims=True)
        own_ref[...] = gates_ref[pl.ds((4 * s_ref[0] + t_ref[0]) * ROWS, ROWS), :]
        total[...] = jnp.zeros_like(total)

    gate_up = nn(rows_ref[:, :HALF], up0[...]) + nn(rows_ref[:, HALF:], up1[...])
    gate_up_ref[...] = gate_up.astype(BF)
    gates = gates_ref[...]
    for i in range(3):
        gate_part, up_part = gate_up[:, head(i)], gate_up[:, head(3 + i)]
        hidden = gate_part * jax.nn.sigmoid(gate_part) * up_part
        gated_ref[:, head(i)] = (hidden * gate_column(gates, s_ref[0], 3 * step + i)).astype(BF)
    gated = gated_ref[...]
    total[:, :HALF] += nt(gated, down0[...])
    total[:, HALF:] += nt(gated, down1[...])

    @pl.when(step == STEPS - 1)
    def _():
        part[...] = total[...].astype(BF)


def fixed(*shape):
    return pl.BlockSpec(shape, lambda j: (0,) * len(shape))


def by_step(rows, columns, first=0):
    return pl.BlockSpec((rows, columns), lambda j: (0, first + j))


def ffn_weight_specs():
    return [by_step(HALF, 2 * STEP)] * 2 + [by_step(HALF, STEP, UP // STEP)] * 2


def ffn_forward(s, t, rows, router, mask, weights):
    return run(
        ffn_forward_kernel,
        [
            shaped((ROUTES, D)),
            shaped((ROUTES, E), F32),
            shaped((ROWS, E), F32),
            shaped((ROUTES, UP)),
            shaped((ROUTES, DOWN)),
        ],
        [s, t, rows, router, mask, weights[0], weights[1], weights[0], weights[1]],
        flops=2 * ROUTES * D * PIECE,
        in_specs=[SMEM, SMEM, fixed(ROUTES, D), fixed(E, D), fixed(ROUTES, E)] + ffn_weight_specs(),
        out_specs=[fixed(ROUTES, D), fixed(ROUTES, E), fixed(ROWS, E)]
        + [by_step(ROUTES, 2 * STEP), by_step(ROUTES, STEP)],
        grid=(STEPS,),
        scratch=[pltpu.VMEM((ROUTES, D), F32)],
    )


def ffn_backward_kernel(s_ref, rows_ref, gates_ref, gate_up_ref, up0, up1, down0, down1, *refs):
    step = pl.program_id(0)
    part, grad_ref, total, products = refs

    @pl.when(step == 0)
    def _():
        total[...] = jnp.zeros_like(total)
        products[...] = jnp.zeros_like(products)

    hidden_grad = nn(rows_ref[:, :HALF], down0[...]) + nn(rows_ref[:, HALF:], down1[...])
    gates = gates_ref[...]
    lane = lax.broadcasted_iota(jnp.int32, (ROUTES, HD), 1)
    for i in range(3):
        number = 3 * step + i
        gate_part = gate_up_ref[:, head(i)].astype(F32)
        up_part = gate_up_ref[:, head(3 + i)].astype(F32)
        sigmoid = jax.nn.sigmoid(gate_part)
        silu = gate_part * sigmoid
        upstream = hidden_grad[:, head(i)]
        product = jnp.sum(silu * up_part * upstream, axis=1, keepdims=True)
        at = jnp.where(number < HALF_E, s_ref[0] * HALF_E + number, -1)
        products[...] = jnp.where(lane == at, product, products[...])
        upstream = upstream * gate_column(gates, s_ref[0], number)
        gate_grad = upstream * up_part * sigmoid * (1.0 + gate_part * (1.0 - sigmoid))
        grad_ref[:, head(i)] = gate_grad.astype(BF)
        grad_ref[:, head(3 + i)] = (upstream * silu).astype(BF)
    grad = grad_ref[...]
    total[:, :HALF] += nt(grad, up0[...])
    total[:, HALF:] += nt(grad, up1[...])

    @pl.when(step == STEPS - 1)
    def _():
        whole = products[...]
        high = whole.astype(BF).astype(F32)
        extra = high + pltpu.roll(whole - high, E, 1)
        part[:, :D] = total[...].astype(BF)
        part[:, D:] = extra.astype(BF)


def ffn_backward(s, rows, gates, gate_up, weights):
    return run(
        ffn_backward_kernel,
        [shaped((ROUTES, WIDE)), shaped((ROUTES, UP))],
        [s, rows, gates, gate_up, weights[0], weights[1], weights[0], weights[1]],
        flops=2 * ROUTES * D * PIECE,
        in_specs=[SMEM, fixed(ROUTES, D), fixed(ROUTES, E), by_step(ROUTES, 2 * STEP)]
        + ffn_weight_specs(),
        out_specs=[fixed(ROUTES, WIDE), by_step(ROUTES, 2 * STEP)],
        grid=(STEPS,),
        scratch=[pltpu.VMEM((ROUTES, D), F32), pltpu.VMEM((ROUTES, HD), F32)],
    )


def ffn_weights_kernel(rows, grad_rows, gate_up_grad, gated, *refs):
    step = pl.program_id(0)
    out = refs[-1]

    def store(total):
        if len(refs) > 1:
            total = total + refs[0][...].astype(F32)
        out[...] = total.astype(BF)

    @pl.when(step < 2)
    def _():
        store(tn(rows[...], gate_up_grad[...]))

    @pl.when(step == 2)
    def _():
        store(tn(grad_rows[...], gated[...]))


def ffn_weights(half, rows, grad_rows, gate_up_grad, gated, *other):
    cut = pl.BlockSpec((ROUTES, HALF), lambda j: (0, half))
    third = pl.BlockSpec((ROUTES, DOWN), lambda j: (0, jnp.minimum(j, 1)))
    return run(
        ffn_weights_kernel,
        [shaped((HALF, PIECE))],
        [rows, grad_rows, gate_up_grad, gated, *other],
        flops=2 * ROUTES * HALF * PIECE,
        in_specs=[cut, cut, third, fixed(ROUTES, DOWN)] + [by_step(HALF, DOWN)] * len(other),
        out_specs=[by_step(HALF, DOWN)],
        grid=(3,),
    )[0]


def mid_kernel(hidden, gain, *refs):
    mid_ref, normed_ref, copies = refs[-3:]
    mid = hidden[...].astype(F32) + add_up(refs[:-3])
    mid_ref[...] = mid
    normed = (mid * rms_factor(mid) * gain[...]).astype(BF)
    normed_ref[...] = normed
    for index in range(8):
        copies[block(index), :] = normed


def result_kernel(mid, got, out):
    out[...] = (mid[...] + add_blocks(got)).astype(BF)


def mid_backward_kernel(mid, own_gates, out_grad, gain, router, normed, got, *refs):
    mid_grad_ref, low_ref, gain_grad, router_grad = refs
    total = add_blocks(got)
    extra = total[:, D:]
    gate_grad = (extra + pltpu.roll(extra, HD - E, 1))[:, :E]
    own = own_gates[...]
    logits_grad = own * (gate_grad - jnp.sum(own * gate_grad, axis=1, keepdims=True))
    logits_grad = logits_grad.astype(BF)
    upstream = total[:, :D] + nn(logits_grad, router[...])
    grad, gain_grad[...] = norm_backward(mid[...], gain[...], upstream)
    router_grad[...] = tn(logits_grad, normed[...])
    mid_grad = out_grad[...].astype(F32) + grad
    mid_grad_ref[...] = mid_grad
    low_ref[...] = mid_grad.astype(BF)


def hidden_backward_kernel(hidden, gain, mid_grad, *refs):
    out, gain_grad, copies = refs[-3:]
    grad, gain_grad[...] = norm_backward(hidden[...].astype(F32), gain[...], add_up(refs[:-3]))
    low = (mid_grad[...] + grad).astype(BF)
    out[...] = low
    for index in range(8):
        copies[block(index), :] = low


def send_home(blocks, home):
    blocks = blocks.reshape(2, DBLK, -1)
    beside = move(blocks[1], SIDE, lambda s, x: (s, x + 1), lambda s, x: s == home)
    straight = move(blocks[0], SIDE, lambda s, x: (s + 1, x), lambda s, x: s != home)
    across = move(blocks[1], SIDE, lambda s, x: (s + 1, x + 1), lambda s, x: s != home)
    return blocks[0], beside, straight, across


def from_home(sent):
    own, beside, straight, across = [x.astype(F32) for x in sent]
    return own + beside, straight + across


def swap_core(part):
    return move(part, CORE, lambda c: (1 - c,))


def sum_row(part):
    return lax.psum_scatter(part, "z", scatter_dimension=0, tiled=True)


def gather_row(part):
    return lax.all_gather(part, "z", axis=0, tiled=True)


def per_device(
    tokens,
    cotangent,
    route_experts,
    route_slots,
    gain_attn,
    w_query,
    w_key,
    w_value,
    w_out,
    gain_ffn,
    w_router,
    w_shared_in,
    w_shared_down,
    w_expert_in,
    w_expert_down,
):
    s = lax.axis_index("section")
    xhi = lax.axis_index("xhi")
    core = lax.axis_index("core")
    z = lax.axis_index("z")
    t = lax.axis_index("tensor")
    first = s == 0
    s_arg = s.astype(jnp.int32)[None]
    t_arg = t.astype(jnp.int32)[None]

    small = jnp.concatenate(
        [gain_attn[0][:, None], gain_ffn[0][:, None], w_router[0], jnp.zeros((24, 110), BF)], axis=1
    )
    small = rolled(jnp.stack(tensor_gather(small)), (4 - t) % 4).reshape(DBLK, HD)
    att_piece = jnp.concatenate([w_query[0], w_key[0], w_value[0], w_out[0].T, small], axis=1)

    expert_in = w_expert_in[0].reshape(DBLK, 2, HALF_E, 2, HD)
    shared_in = w_shared_in[0].reshape(DBLK, 2, 2, HD)
    expert_down = w_expert_down[0].transpose(2, 0, 1).reshape(DBLK, 2, HALF_E * HD)
    shared_down = w_shared_down[0].T.reshape(DBLK, 2, HD)

    def ffn_piece(part):
        up = jnp.concatenate([expert_in[:, part], shared_in[:, None, :, part]], axis=1)
        up = up.reshape(DBLK, STEPS, 3, 2, HD).swapaxes(2, 3).reshape(DBLK, UP)
        return jnp.concatenate([up, expert_down[:, part], shared_down[:, part]], axis=1)

    ffn_own = jnp.where(first, ffn_piece(0), ffn_piece(1))
    ffn_other = jnp.where(first, ffn_piece(1), ffn_piece(0))

    att_beside = move(att_piece, SIDE, lambda s, x: (s, x + 1))
    att_straight = move(att_piece, SIDE, lambda s, x: (s + 1, x))
    att_across = move(att_piece, SIDE, lambda s, x: (s + 1, x + 1))
    att_beside, att_straight, att_across, ffn_own, ffn_other = together(
        att_beside, att_straight, att_across, ffn_own, ffn_other
    )
    att_same = jnp.concatenate([att_piece, att_beside], axis=0)
    att_else = jnp.concatenate([att_straight, att_across], axis=0)
    att_pairs = [jnp.where(first, att_same, att_else), jnp.where(first, att_else, att_same)]
    ffn_straight = move(ffn_other, SIDE, lambda s, x: (s + 1, x))
    ffn_across = move(ffn_other, SIDE, lambda s, x: (s + 1, x + 1))
    ffn_beside0 = move(ffn_own, SIDE, lambda s, x: (s, x + 1), lambda s, x: s == 0)
    ffn_else = jnp.concatenate([ffn_straight, ffn_across], axis=0)
    ffn_pair0 = jnp.where(first, jnp.concatenate([ffn_own, ffn_beside0], axis=0), ffn_else)

    att_row0 = gather_row(att_pairs[0])
    ffn_row0 = gather_row(ffn_pair0)

    place = jnp.arange(D, dtype=jnp.int32)
    at_core = (place // HALF + core) % 2
    at_z = (place // (2 * DBLK)) % 4
    at_x = (place // DBLK + xhi) % 2
    column = at_x * HALF + at_z * (2 * DBLK) + at_core * DBLK + place % DBLK
    order = (place[:, None] == column[None, :]).astype(BF)

    own_tokens = lax.dynamic_index_in_dim(tokens, s, 0, keepdims=False)
    own_cotangent = lax.dynamic_index_in_dim(cotangent, s, 0, keepdims=False)
    own_rows = nn(jnp.concatenate([own_tokens, own_cotangent], axis=0), order).astype(BF)
    hidden_blocks = tensor_gather(own_rows[:ROWS])
    own_cotangent = own_rows[ROWS:]

    named = jnp.sum((route_experts[0][:, :, :, None] == jnp.arange(E)).astype(F32), axis=2)
    named = named.astype(BF).reshape(ROUTES, E)
    named_else = move(named, SECTION, lambda s: (s + 1,))

    masks = [jnp.where(s == layer, named, named_else).astype(F32) for layer in (0, 1)]

    att_row0, masks[0], masks[1], *hidden_blocks = together(
        att_row0, masks[0], masks[1], *hidden_blocks
    )
    att_w = [(att_row0, swap_core(att_row0)), None]
    ffn_w = [None, None]
    layer_values = []
    kept = []
    for layer in (0, 1):
        parts, att_saved = attention_forward(t_arg, hidden_blocks, att_w[layer])
        normed, *att_saved, small = att_saved
        attn_gain, ffn_gain, router = small[0:1], small[1:2], small[2 : 2 + E].astype(BF)
        mid, normed_ffn, copies = run(
            mid_kernel,
            [shaped((ROWS, D), F32), shaped((ROWS, D)), shaped((ROUTES, D))],
            [hidden_blocks[0], ffn_gain, parts[0], *tensor_send(parts)],
        )
        rows = group_exchange(copies)
        if layer == 0:
            normed, own_cotangent = together(normed, own_cotangent)
            grad_rows = group_exchange(jnp.tile(own_cotangent, (8, 1)))
            ffn_row0, rows, grad_rows, att_pair1, ffn_own, ffn_else = together(
                ffn_row0, rows, grad_rows, att_pairs[1], ffn_own, ffn_else
            )
            ffn_w[0] = (ffn_row0, swap_core(ffn_row0))
            ffn_beside1 = move(ffn_own, SIDE, lambda s, x: (s, x + 1), lambda s, x: s == 1)
            ffn_pair1 = jnp.where(first, ffn_else, jnp.concatenate([ffn_own, ffn_beside1], axis=0))
            att_row1 = gather_row(att_pair1)
            ffn_row1 = gather_row(ffn_pair1)
        else:
            ffn_row1, mid = together(ffn_row1, mid)
            ffn_w[1] = (ffn_row1, swap_core(ffn_row1))
        part, gates, own_gates, gate_up, gated = ffn_forward(
            s_arg, t_arg, rows, router, masks[layer], ffn_w[layer]
        )
        result = run(result_kernel, [shaped((ROWS, D))], [mid, group_exchange(part)])[0]
        layer_values.append(result)
        kept.append((hidden_blocks[0], attn_gain, normed, *att_saved))
        kept.append((mid, ffn_gain, router, normed_ffn, rows, gates, own_gates, gate_up, gated))
        if layer == 0:
            hidden_blocks = tensor_gather(result)
            att_row1, own_gates = together(att_row1, own_gates)
            kept[1] = (*kept[1][:6], own_gates, gate_up, gated)
            att_w[1] = (att_row1, swap_core(att_row1))

    in_grads = [None, None]
    small_grads = [None, None]
    ffn_sums = [None, None]
    att_sums = [None, None]
    out_low = own_cotangent
    for layer in (1, 0):
        hidden, attn_gain, normed, qkv, probs, attended = kept[2 * layer]
        mid, ffn_gain, router, normed_ffn, rows, gates, own_gates, gate_up, gated = kept[2 * layer + 1]
        part, gate_up_grad = ffn_backward(s_arg, grad_rows, gates, gate_up, ffn_w[layer])
        ffn_parts = (rows, grad_rows, gate_up_grad, gated)
        other = None
        if layer == 0:
            part, other = together(part, ffn_weights(1, *ffn_parts))
            other = swap_core(other)
        mid_grad, mid_low, grad_gain_ffn, grad_router = run(
            mid_backward_kernel,
            [
                shaped((ROWS, D), F32),
                shaped((ROWS, D)),
                shaped((1, D), F32),
                shaped((E, D), F32),
            ],
            [mid, own_gates, out_low, ffn_gain, router, normed_ffn, group_exchange(part)],
        )
        mid_blocks = tensor_gather(mid_low)
        if layer == 1:
            *mid_blocks, other = together(*mid_blocks, ffn_weights(1, *ffn_parts))
            other = swap_core(other)
        else:
            gate_up_grad, ffn_sums[1] = together(gate_up_grad, ffn_sums[1])
            own = ffn_weights(0, rows, grad_rows, gate_up_grad, gated, other)
            *mid_blocks, own = together(*mid_blocks, own)
            ffn_sums[0] = sum_row(own)
        parts, mid_rows, qkv_grad = attention_backward(mid_blocks, att_w[layer], qkv, probs)
        got = tensor_send(parts)
        att_parts = (normed, mid_rows, qkv_grad, attended)
        att_other = attention_weights(1, *att_parts)
        if layer == 1:
            own = ffn_weights(0, *ffn_parts, other)
            *got, att_other, own = together(*got, att_other, own)
            ffn_sums[1] = sum_row(own)
        else:
            *got, att_other = together(*got, att_other)
        out_low, grad_gain_attn, copies = run(
            hidden_backward_kernel,
            [shaped((ROWS, D)), shaped((1, D), F32), shaped((ROUTES, D))],
            [hidden, attn_gain, mid_grad, parts[0], *got],
        )
        in_grads[layer] = out_low
        small_grads[layer] = jnp.concatenate([grad_gain_attn, grad_gain_ffn, grad_router], axis=0)
        att_own = attention_weights(0, *att_parts, swap_core(att_other))
        if layer == 1:
            grad_rows, att_own = together(group_exchange(copies), att_own)
            att_sums[1] = sum_row(att_own)
    att_blocks = rolled(att_own.reshape(4, 2 * DBLK, ATT), z)
    total = att_blocks[0].astype(F32)
    for k in (1, 2, 3):
        total = total + move(att_blocks[k], ROW, lambda at, k=k: (at + k,)).astype(F32)
    att_sums[0] = total.astype(BF)
    out_low, ffn_sums[1], att_sums[1] = together(in_grads[0], ffn_sums[1], att_sums[1])
    in_grads[0] = out_low
    ffn_home = [None, send_home(ffn_sums[1], 1)]
    att_home = [None, send_home(att_sums[1], 1)]
    att_home[0] = send_home(att_sums[0], 0)
    ffn_home[0] = send_home(ffn_sums[0], 0)

    def both_sequences(values):
        low = nt(jnp.concatenate(values, axis=0), order).astype(BF).reshape(2, ROWS, D)
        mine = jnp.where(first, low[0], low[1])
        got = move(jnp.where(first, low[1], low[0]), SECTION, lambda s: (s + 1,))
        return jnp.where(first, jnp.stack([mine, got]), jnp.stack([got, mine]))[None]

    values_out = both_sequences(layer_values)
    grads_in = both_sequences(in_grads)

    att_home = [sum(from_home(sent)) for sent in att_home]
    ffn_home = [from_home(sent) for sent in ffn_home]
    att = jnp.where(first, att_home[0], att_home[1])
    ffn_mine = jnp.where(first, ffn_home[0][0], ffn_home[1][0])
    ffn_got = jnp.where(first, ffn_home[0][1], ffn_home[1][1])
    ffn_parts = (jnp.where(first, ffn_mine, ffn_got), jnp.where(first, ffn_got, ffn_mine))

    values = jnp.concatenate(small_grads, axis=0).T.reshape(2, 4, 2, DBLK, 2 * (2 + E))
    values = values[0] + move(values[1], CORE, lambda c: (1 - c,))
    values = rolled(values, z)
    total = values[0]
    for k in (1, 2, 3):
        total = total + move(values[k], ROW, lambda at, k=k: (at + k,))
    total = total[0] + move(total[1], ("xhi",), lambda x: (x + 1,))
    halves = total.reshape(DBLK, 2, 2 + E).swapaxes(0, 1)
    mine = jnp.where(first, halves[0], halves[1])
    theirs = jnp.where(first, halves[1], halves[0])
    total = mine + move(theirs, SECTION, lambda s: (s + 1,))
    total = rolled(total.reshape(4, DBLK // 4, 2 + E), t)
    small_sum = total[0]
    for got in tensor_send([total[k] for k in range(4)]):
        small_sum = small_sum + got

    ups, downs = [], []
    for part in ffn_parts:
        up = part[:, :UP].reshape(DBLK, STEPS, 2, 3, HD).swapaxes(2, 3)
        ups.append(up.reshape(DBLK, BLOCKS, 2, HD))
        downs.append(part[:, UP:].reshape(DBLK, BLOCKS, HD))
    grad_expert_in = jnp.concatenate([up[:, :HALF_E] for up in ups], axis=1)
    grad_shared_in = jnp.concatenate([up[:, HALF_E] for up in ups], axis=2)
    grad_expert_down = jnp.concatenate([down[:, :HALF_E] for down in downs], axis=1)
    grad_shared_down = jnp.concatenate([down[:, HALF_E] for down in downs], axis=1)
    return (
        values_out,
        grads_in,
        small_sum[:, 0][None],
        att[:, : GROUPS * HD][None],
        att[:, KEYS][None],
        att[:, VALUES][None],
        att[:, QKV:].T[None],
        small_sum[:, 1][None],
        small_sum[:, 2:][None],
        grad_shared_in[None],
        grad_shared_down.T[None],
        grad_expert_in[None],
        grad_expert_down.transpose(1, 2, 0)[None],
    )


def solution(mesh):
    split = Mesh(
        mesh.devices.reshape(2, 2, 4, 2, 4), ("section", "xhi", "z", "core", "tensor")
    )
    dp = ("xhi", "z", "core")
    both = dp + ("tensor",)
    placed = (
        P(dp, "tensor", None),
        P(dp, "tensor", None),
        P("section", dp, None, None),
        P("section", dp, None, None),
        P("section", both),
        P("section", dp, "tensor"),
        P("section", dp, "tensor"),
        P("section", dp, "tensor"),
        P("section", "tensor", dp),
        P("section", both),
        P("section", both, None),
        P("section", dp, None, "tensor"),
        P("section", "tensor", dp),
        P("section", dp, None, None, "tensor"),
        P("section", None, "tensor", dp),
    )
    return jax.shard_map(
        per_device,
        mesh=split,
        in_specs=placed,
        out_specs=(
            P("section", dp, "tensor", None),
            P("section", dp, "tensor", None),
            P("section", both),
            P("section", dp, "tensor"),
            P("section", dp, "tensor"),
            P("section", dp, "tensor"),
            P("section", "tensor", dp),
            P("section", both),
            P("section", both, None),
            P("section", dp, None, "tensor"),
            P("section", "tensor", dp),
            P("section", dp, None, None, "tensor"),
            P("section", None, "tensor", dp),
        ),
        check_vma=False,
    )
```

```python
import jax
import jax.numpy as jnp
from jax import lax
from jax.experimental import pallas as pl
from jax.experimental.pallas import tpu as pltpu
from jax.sharding import Mesh
from jax.sharding import PartitionSpec as P

D = 1536
HD = 128
E = 16
HALF_E = 8
GROUPS = 3
LEN = 256
ROWS = 64
DBLK = 96
HALF = D // 2
ROUTES = 2 * LEN

NORM_EPSILON = 1e-05
MASK_VALUE = -1e30
SCALE = HD**-0.5

BF = jnp.bfloat16
F32 = jnp.float32

QKV = 640
ATT = 1024
ATT_PAD = 1152
BLOCKS = 9
STEPS = 3
STEP = 3 * HD
UP = BLOCKS * 256
DOWN = BLOCKS * 128
PIECE = UP + DOWN
WIDE = D + HD
SMALL = 24

SECTION = ("section",)
TENSOR = ("tensor",)
GROUP = ("section", "tensor")
CORE = ("core",)
ROW = ("z",)
SIDE = ("section", "xhi")


def dot(a, b, contract):
    return lax.dot_general(a, b, ((contract[:1], contract[1:]), ((), ())), preferred_element_type=F32)


def nn(a, b):
    return dot(a, b, (1, 0))


def nt(a, b):
    return dot(a, b, (1, 1))


def tn(a, b):
    return dot(a, b, (0, 0))


def move(block, axes, target, only=None):
    sizes = [lax.axis_size(axis) for axis in axes]
    pairs = []

    def flat(place):
        index = 0
        for size, at in zip(sizes, place):
            index = index * size + at % size
        return index

    def walk(place):
        if len(place) == len(sizes):
            if only is None or only(*place):
                pairs.append((flat(place), flat(target(*place))))
            return
        for at in range(sizes[len(place)]):
            walk(place + (at,))

    walk(())
    return lax.ppermute(block, axes, pairs)

VMEM = pl.BlockSpec(memory_space=pltpu.VMEM)
SMEM = pl.BlockSpec(memory_space=pltpu.SMEM)


def shaped(shape, dtype=BF):
    return jax.ShapeDtypeStruct(shape, dtype)


def run(kernel, outs, operands, scalars=0, flops=0, in_specs=None, out_specs=None, grid=(), scratch=()):
    if in_specs is None:
        in_specs = [SMEM] * scalars + [VMEM] * (len(operands) - scalars)
    if out_specs is None:
        out_specs = [VMEM] * len(outs)
    moved = sum(x.size * x.dtype.itemsize for x in list(operands) + list(outs))
    return pl.pallas_call(
        kernel,
        out_shape=list(outs),
        in_specs=in_specs,
        out_specs=out_specs,
        grid=grid,
        scratch_shapes=list(scratch),
        compiler_params=pltpu.CompilerParams(vmem_limit_bytes=48 * 1024 * 1024),
        cost_estimate=pl.CostEstimate(flops=flops, bytes_accessed=moved, transcendentals=0),
    )(*operands)


def together(*values):
    return lax.optimization_barrier(values)


def tensor_gather(rows):
    return [rows] + [move(rows, TENSOR, lambda t, k=k: (t - k,)) for k in (1, 2, 3)]


def tensor_send(parts):
    return [move(parts[k], TENSOR, lambda t, k=k: (t + k,)) for k in (1, 2, 3)]


def group_exchange(rows):
    return lax.all_to_all(rows, GROUP, 0, 0, tiled=True)


def rolled(stacked, shift):
    n = stacked.shape[0]
    return lax.dynamic_slice_in_dim(jnp.concatenate([stacked, stacked], axis=0), shift, n, 0)


def rms_factor(rows):
    return lax.rsqrt(jnp.mean(rows * rows, axis=-1, keepdims=True) + NORM_EPSILON)


def norm_backward(rows, gain, upstream):
    factor = rms_factor(rows)
    unit = rows * factor
    scaled = upstream * gain
    grad = factor * (scaled - unit * jnp.mean(scaled * unit, axis=-1, keepdims=True))
    return grad, jnp.sum(upstream * unit, axis=0, keepdims=True)


def add_up(refs):
    total = refs[0][...].astype(F32)
    for ref in refs[1:]:
        total = total + ref[...].astype(F32)
    return total


def block(index):
    return slice(index * ROWS, (index + 1) * ROWS)


def add_blocks(ref):
    total = ref[block(0), :].astype(F32)
    for index in range(1, 8):
        total = total + ref[block(index), :].astype(F32)
    return total


def head(index):
    return slice(index * HD, (index + 1) * HD)


KEYS = head(GROUPS)
VALUES = head(GROUPS + 1)


def attention_forward_kernel(t_ref, *refs):
    hidden, (gain, w0, w1) = refs[:4], refs[4:7]
    parts, (normed_ref, qkv_ref, probs_ref, attended_ref) = refs[7:11], refs[11:]
    for index, ref in enumerate(hidden):
        rows = ref[...].astype(F32)
        normed_ref[block(index), :] = (rows * rms_factor(rows) * gain[...]).astype(BF)
    normed = normed_ref[...]
    qkv = nn(normed[:, :HALF], w0[:, :QKV]) + nn(normed[:, HALF:], w1[:, :QKV])
    qkv = qkv.astype(BF)
    qkv_ref[...] = qkv

    def position(axis):
        return (t_ref[0] * ROWS + lax.broadcasted_iota(jnp.int32, (LEN, LEN), axis)) & (LEN - 1)

    causal = position(1) <= position(0)
    for g in range(GROUPS):
        scores = jnp.where(causal, nt(qkv[:, head(g)], qkv[:, KEYS]) * SCALE, MASK_VALUE)
        shifted = jnp.exp(scores - jnp.max(scores, axis=-1, keepdims=True))
        probs = (shifted / jnp.sum(shifted, axis=-1, keepdims=True)).astype(BF)
        probs_ref[g] = probs
        attended_ref[:, head(g)] = nn(probs, qkv[:, VALUES]).astype(BF)
    attended = attended_ref[...]
    for at, w in ((0, w0), (HALF, w1)):
        out = nt(attended, w[:, QKV:ATT]).astype(BF)
        for index, part in enumerate(parts):
            part[:, at : at + HALF] = out[block(index)]


def attention_forward(t, hidden_blocks, gain, weights):
    outs = [shaped((ROWS, D))] * 4
    outs += [shaped((LEN, D)), shaped((LEN, QKV)), shaped((GROUPS, LEN, LEN)), shaped((LEN, STEP))]
    flops = 2 * LEN * D * ATT + 4 * GROUPS * LEN * LEN * HD
    got = run(attention_forward_kernel, outs, [t, *hidden_blocks, gain, *weights], 1, flops)
    return got[:4], got[4:]


def attention_backward_kernel(*refs):
    grads, (w0, w1, qkv_ref, probs_ref) = refs[:4], refs[4:8]
    parts, (rows_ref, qkv_grad_ref) = refs[8:12], refs[12:]
    for index, ref in enumerate(grads):
        rows_ref[block(index), :] = ref[...]
    rows = rows_ref[...]
    attended_grad = nn(rows[:, :HALF], w0[:, QKV:ATT]) + nn(rows[:, HALF:], w1[:, QKV:ATT])
    attended_grad = attended_grad.astype(BF)
    qkv = qkv_ref[...]
    key_grad = jnp.zeros((LEN, HD), F32)
    value_grad = jnp.zeros((LEN, HD), F32)
    for g in range(GROUPS):
        probs = probs_ref[g]
        upstream = attended_grad[:, head(g)]
        value_grad = value_grad + tn(probs, upstream)
        prob_grad = nt(upstream, qkv[:, VALUES])
        wide = probs.astype(F32)
        score_grad = wide * (prob_grad - jnp.sum(wide * prob_grad, axis=-1, keepdims=True))
        score_grad = (score_grad * SCALE).astype(BF)
        qkv_grad_ref[:, head(g)] = nn(score_grad, qkv[:, KEYS]).astype(BF)
        key_grad = key_grad + tn(score_grad, qkv[:, head(g)])
    qkv_grad_ref[:, KEYS] = key_grad.astype(BF)
    qkv_grad_ref[:, VALUES] = value_grad.astype(BF)
    qkv_grad = qkv_grad_ref[...]
    for at, w in ((0, w0), (HALF, w1)):
        out = nt(qkv_grad, w[:, :QKV]).astype(BF)
        for index, part in enumerate(parts):
            part[:, at : at + HALF] = out[block(index)]


def attention_backward(grad_blocks, weights, qkv, probs):
    outs = [shaped((ROWS, D))] * 4 + [shaped((LEN, D)), shaped((LEN, QKV))]
    flops = 2 * LEN * D * ATT + 10 * GROUPS * LEN * LEN * HD
    got = run(attention_backward_kernel, outs, [*grad_blocks, *weights, qkv, probs], 0, flops)
    return got[:4], got[4], got[5]


def attention_weights_kernel(normed, rows, qkv_grad, attended, *refs):
    out = refs[-1]
    for columns, left, right in (
        (slice(0, QKV), normed, qkv_grad),
        (slice(QKV, ATT), rows, attended),
    ):
        total = tn(left[...], right[...])
        if len(refs) > 1:
            total = total + refs[0][:, columns].astype(F32)
        out[:, columns] = total.astype(BF)


def attention_weights(half, normed, rows, qkv_grad, attended, *other):
    def full(*shape):
        return pl.BlockSpec(shape, lambda i: (0, 0))

    cut = pl.BlockSpec((LEN, HALF), lambda i: (0, half))
    in_specs = [cut, cut, full(LEN, QKV), full(LEN, STEP)] + [full(HALF, ATT)] * len(other)
    return run(
        attention_weights_kernel,
        [shaped((HALF, ATT))],
        [normed, rows, qkv_grad, attended, *other],
        flops=2 * HALF * LEN * ATT,
        in_specs=in_specs,
        out_specs=[full(HALF, ATT)],
        grid=(1,),
    )[0]


def gate_column(gates, section, number):
    lane = lax.broadcasted_iota(jnp.int32, gates.shape, 1)
    picked = jnp.where(lane == section * HALF_E + number, gates, 0.0)
    return jnp.where(number == HALF_E, 1.0, jnp.sum(picked, axis=1, keepdims=True))


def ffn_forward_kernel(s_ref, t_ref, rows_ref, router, mask_ref, up0, up1, down0, down1, *refs):
    step = pl.program_id(0)
    part, gates_ref, own_ref, gate_up_ref, gated_ref, total = refs

    @pl.when(step == 0)
    def _():
        logits = nt(rows_ref[...], router[...])
        named = mask_ref[...] > 0.5
        top = jnp.max(jnp.where(named, logits, MASK_VALUE), axis=-1, keepdims=True)
        shifted = jnp.where(named, jnp.exp(jnp.where(named, logits - top, 0.0)), 0.0)
        gates_ref[...] = shifted / jnp.sum(shifted, axis=-1, keepdims=True)
        own_ref[...] = gates_ref[pl.ds((4 * s_ref[0] + t_ref[0]) * ROWS, ROWS), :]
        total[...] = jnp.zeros_like(total)

    gate_up = nn(rows_ref[:, :HALF], up0[...]) + nn(rows_ref[:, HALF:], up1[...])
    gate_up_ref[...] = gate_up.astype(BF)
    gates = gates_ref[...]
    for i in range(3):
        gate_part, up_part = gate_up[:, head(i)], gate_up[:, head(3 + i)]
        hidden = gate_part * jax.nn.sigmoid(gate_part) * up_part
        gated_ref[:, head(i)] = (hidden * gate_column(gates, s_ref[0], 3 * step + i)).astype(BF)
    gated = gated_ref[...]
    total[:, :HALF] += nt(gated, down0[...])
    total[:, HALF:] += nt(gated, down1[...])

    @pl.when(step == STEPS - 1)
    def _():
        part[...] = total[...].astype(BF)


def fixed(*shape):
    return pl.BlockSpec(shape, lambda j: (0,) * len(shape))


def by_step(rows, columns, first=0):
    return pl.BlockSpec((rows, columns), lambda j: (0, first + j))


def ffn_weight_specs():
    return [by_step(HALF, 2 * STEP)] * 2 + [by_step(HALF, STEP, UP // STEP)] * 2


def ffn_forward(s, t, rows, router, mask, weights):
    return run(
        ffn_forward_kernel,
        [
            shaped((ROUTES, D)),
            shaped((ROUTES, E), F32),
            shaped((ROWS, E), F32),
            shaped((ROUTES, UP)),
            shaped((ROUTES, DOWN)),
        ],
        [s, t, rows, router, mask, weights[0], weights[1], weights[0], weights[1]],
        flops=2 * ROUTES * D * PIECE,
        in_specs=[SMEM, SMEM, fixed(ROUTES, D), fixed(E, D), fixed(ROUTES, E)] + ffn_weight_specs(),
        out_specs=[fixed(ROUTES, D), fixed(ROUTES, E), fixed(ROWS, E)]
        + [by_step(ROUTES, 2 * STEP), by_step(ROUTES, STEP)],
        grid=(STEPS,),
        scratch=[pltpu.VMEM((ROUTES, D), F32)],
    )


def ffn_backward_kernel(s_ref, rows_ref, gates_ref, gate_up_ref, up0, up1, down0, down1, *refs):
    step = pl.program_id(0)
    part, grad_ref, total, products = refs

    @pl.when(step == 0)
    def _():
        total[...] = jnp.zeros_like(total)
        products[...] = jnp.zeros_like(products)

    hidden_grad = nn(rows_ref[:, :HALF], down0[...]) + nn(rows_ref[:, HALF:], down1[...])
    gates = gates_ref[...]
    lane = lax.broadcasted_iota(jnp.int32, (ROUTES, HD), 1)
    for i in range(3):
        number = 3 * step + i
        gate_part = gate_up_ref[:, head(i)].astype(F32)
        up_part = gate_up_ref[:, head(3 + i)].astype(F32)
        sigmoid = jax.nn.sigmoid(gate_part)
        silu = gate_part * sigmoid
        upstream = hidden_grad[:, head(i)]
        product = jnp.sum(silu * up_part * upstream, axis=1, keepdims=True)
        at = jnp.where(number < HALF_E, s_ref[0] * HALF_E + number, -1)
        products[...] = jnp.where(lane == at, product, products[...])
        upstream = upstream * gate_column(gates, s_ref[0], number)
        gate_grad = upstream * up_part * sigmoid * (1.0 + gate_part * (1.0 - sigmoid))
        grad_ref[:, head(i)] = gate_grad.astype(BF)
        grad_ref[:, head(3 + i)] = (upstream * silu).astype(BF)
    grad = grad_ref[...]
    total[:, :HALF] += nt(grad, up0[...])
    total[:, HALF:] += nt(grad, up1[...])

    @pl.when(step == STEPS - 1)
    def _():
        whole = products[...]
        high = whole.astype(BF).astype(F32)
        extra = high + pltpu.roll(whole - high, E, 1)
        part[:, :D] = total[...].astype(BF)
        part[:, D:] = extra.astype(BF)


def ffn_backward(s, rows, gates, gate_up, weights):
    return run(
        ffn_backward_kernel,
        [shaped((ROUTES, WIDE)), shaped((ROUTES, UP))],
        [s, rows, gates, gate_up, weights[0], weights[1], weights[0], weights[1]],
        flops=2 * ROUTES * D * PIECE,
        in_specs=[SMEM, fixed(ROUTES, D), fixed(ROUTES, E), by_step(ROUTES, 2 * STEP)]
        + ffn_weight_specs(),
        out_specs=[fixed(ROUTES, WIDE), by_step(ROUTES, 2 * STEP)],
        grid=(STEPS,),
        scratch=[pltpu.VMEM((ROUTES, D), F32), pltpu.VMEM((ROUTES, HD), F32)],
    )


def ffn_weights_kernel(rows, grad_rows, gate_up_grad, gated, *refs):
    step = pl.program_id(0)
    out = refs[-1]

    def store(total):
        if len(refs) > 1:
            total = total + refs[0][...].astype(F32)
        out[...] = total.astype(BF)

    @pl.when(step < 2)
    def _():
        store(tn(rows[...], gate_up_grad[...]))

    @pl.when(step == 2)
    def _():
        store(tn(grad_rows[...], gated[...]))


def ffn_weights(half, rows, grad_rows, gate_up_grad, gated, *other):
    cut = pl.BlockSpec((ROUTES, HALF), lambda j: (0, half))
    third = pl.BlockSpec((ROUTES, DOWN), lambda j: (0, jnp.minimum(j, 1)))
    return run(
        ffn_weights_kernel,
        [shaped((HALF, PIECE))],
        [rows, grad_rows, gate_up_grad, gated, *other],
        flops=2 * ROUTES * HALF * PIECE,
        in_specs=[cut, cut, third, fixed(ROUTES, DOWN)] + [by_step(HALF, DOWN)] * len(other),
        out_specs=[by_step(HALF, DOWN)],
        grid=(3,),
    )[0]


def mid_kernel(hidden, gain, *refs):
    mid_ref, normed_ref, copies = refs[-3:]
    mid = hidden[...].astype(F32) + add_up(refs[:-3])
    mid_ref[...] = mid
    normed = (mid * rms_factor(mid) * gain[...]).astype(BF)
    normed_ref[...] = normed
    for index in range(8):
        copies[block(index), :] = normed


def last_kernel(mid, total, out):
    out[...] = (mid[...] + total[...].astype(F32)).astype(BF)


def result_kernel(mid, got, *outs):
    result = (mid[...] + add_blocks(got)).astype(BF)
    for out in outs:
        out[...] = result


def mid_backward_kernel(mid, own_gates, out_grad, gain, router, normed, got, *refs):
    mid_grad_ref, low_ref, small = refs
    total = add_blocks(got)
    extra = total[:, D:]
    gate_grad = (extra + pltpu.roll(extra, HD - E, 1))[:, :E]
    own = own_gates[...]
    logits_grad = own * (gate_grad - jnp.sum(own * gate_grad, axis=1, keepdims=True))
    logits_grad = logits_grad.astype(BF)
    upstream = total[:, :D] + nn(logits_grad, router[...])
    small[...] = jnp.zeros_like(small)
    grad, small[1:2, :] = norm_backward(mid[...], gain[...], upstream)
    small[2 : 2 + E, :] = tn(logits_grad, normed[...])
    mid_grad = out_grad[...].astype(F32) + grad
    mid_grad_ref[...] = mid_grad
    low_ref[...] = mid_grad.astype(BF)


def hidden_backward_kernel(hidden, gain, mid_grad, small_in, *refs):
    out, small, copies = refs[-3:]
    small[...] = small_in[...]
    grad, small[0:1, :] = norm_backward(hidden[...].astype(F32), gain[...], add_up(refs[:-3]))
    low = (mid_grad[...] + grad).astype(BF)
    out[...] = low
    for index in range(8):
        copies[block(index), :] = low


def small_forward_kernel(own, other, out):
    out[:, :HALF] = own[...].astype(F32).T[:64]
    out[:, HALF:] = other[...].astype(F32).T[:64]


def small_backward_kernel(first, second, own, other, both):
    both[...] = jnp.zeros_like(both)
    both[:SMALL, :] = first[...]
    both[32 : 32 + SMALL, :] = second[...]
    own[...] = both[:, :HALF].T.astype(BF)
    other[...] = both[:, HALF:].T.astype(BF)


def final_kernel(s_ref, own, beside, straight, across, *outs):
    query, key, value, out, shared_in, shared_down, expert_in, expert_down, small = outs
    mine = own[...].astype(F32) + beside[...].astype(F32)
    theirs = straight[...].astype(F32) + across[...].astype(F32)
    att = mine[:, PIECE:] + theirs[:, PIECE:]
    query[...] = att[:, : GROUPS * HD]
    key[...] = att[:, KEYS]
    value[...] = att[:, VALUES]
    out[...] = att[:, QKV:ATT]
    small[...] = att[:, ATT:]
    for half in (0, 1):
        part = jnp.where(s_ref[0] == half, mine, theirs)
        for number in range(BLOCKS):
            at = number // 3 * 2 * STEP + number % 3 * HD
            gate_part, up_part = part[:, at : at + HD], part[:, at + STEP : at + STEP + HD]
            down = part[:, UP + number * HD : UP + (number + 1) * HD]
            if number < HALF_E:
                expert = half * HALF_E + number
                expert_in[:, head(2 * expert)] = gate_part
                expert_in[:, head(2 * expert + 1)] = up_part
                expert_down[expert] = down
            else:
                shared_in[:, head(half)] = gate_part
                shared_in[:, head(2 + half)] = up_part
                shared_down[:, head(half)] = down


def swap_core(part):
    return move(part, CORE, lambda c: (1 - c,))


def sum_row(part):
    return lax.psum_scatter(part, "z", scatter_dimension=0, tiled=True)


def gather_row(part):
    return lax.all_gather(part, "z", axis=0, tiled=True)


def per_device(
    tokens,
    cotangent,
    route_experts,
    route_slots,
    gain_attn,
    w_query,
    w_key,
    w_value,
    w_out,
    gain_ffn,
    w_router,
    w_shared_in,
    w_shared_down,
    w_expert_in,
    w_expert_down,
):
    s = lax.axis_index("section")
    xhi = lax.axis_index("xhi")
    core = lax.axis_index("core")
    z = lax.axis_index("z")
    t = lax.axis_index("tensor")
    first = s == 0
    s_arg = s.astype(jnp.int32)[None]
    t_arg = t.astype(jnp.int32)[None]

    small = jnp.concatenate([gain_attn[0][:, None], gain_ffn[0][:, None], w_router[0]], axis=1)
    small = jnp.pad(small, ((0, 0), (0, HD - 2 - E)))
    small = rolled(jnp.stack(tensor_gather(small)), (4 - t) % 4).reshape(DBLK, HD)
    att_piece = jnp.concatenate([w_query[0], w_key[0], w_value[0], w_out[0].T, small], axis=1)

    expert_in = w_expert_in[0].reshape(DBLK, 2, HALF_E, 2, HD)
    shared_in = w_shared_in[0].reshape(DBLK, 2, 2, HD)
    expert_down = w_expert_down[0].transpose(2, 0, 1).reshape(DBLK, 2, HALF_E * HD)
    shared_down = w_shared_down[0].T.reshape(DBLK, 2, HD)

    def ffn_piece(part):
        up = jnp.concatenate([expert_in[:, part], shared_in[:, None, :, part]], axis=1)
        up = up.reshape(DBLK, STEPS, 3, 2, HD).swapaxes(2, 3).reshape(DBLK, UP)
        return jnp.concatenate([up, expert_down[:, part], shared_down[:, part]], axis=1)

    ffn_own = jnp.where(first, ffn_piece(0), ffn_piece(1))
    ffn_other = jnp.where(first, ffn_piece(1), ffn_piece(0))

    named = jnp.sum((route_experts[0][:, :, :, None] == jnp.arange(E)).astype(F32), axis=2)
    named = named.astype(BF).reshape(ROUTES, E)
    named_else = move(named, SECTION, lambda s: (s + 1,))
    att_piece, named_else = together(att_piece, named_else)
    masks = [jnp.where(s == layer, named, named_else).astype(F32) for layer in (0, 1)]

    att_beside = move(att_piece, SIDE, lambda s, x: (s, x + 1))
    att_straight = move(att_piece, SIDE, lambda s, x: (s + 1, x))
    att_across = move(att_piece, SIDE, lambda s, x: (s + 1, x + 1))
    att_straight, ffn_own, ffn_other = together(att_straight, ffn_own, ffn_other)
    att_same = jnp.concatenate([att_piece, att_beside], axis=0)
    att_else = jnp.concatenate([att_straight, att_across], axis=0)
    att_pairs = [jnp.where(first, att_same, att_else), jnp.where(first, att_else, att_same)]
    ffn_straight = move(ffn_other, SIDE, lambda s, x: (s + 1, x))
    ffn_across = move(ffn_other, SIDE, lambda s, x: (s + 1, x + 1))
    ffn_beside0 = move(ffn_own, SIDE, lambda s, x: (s, x + 1), lambda s, x: s == 0)

    smalls = [pair[:, ATT : ATT + 32] for pair in att_pairs]
    att_pair0 = jnp.concatenate(
        [att_pairs[0][:, :ATT], *smalls, jnp.zeros((2 * DBLK, HD - 64), BF)], axis=1
    )
    att_pair1 = att_pairs[1][:, :ATT]
    att_row0 = gather_row(att_pair0)

    place = jnp.arange(D, dtype=jnp.int32)
    at_core = (place // HALF + core) % 2
    at_z = (place // (2 * DBLK)) % 4
    at_x = (place // DBLK + xhi) % 2
    column = at_x * HALF + at_z * (2 * DBLK) + at_core * DBLK + place % DBLK
    order = (place[:, None] == column[None, :]).astype(BF)

    own_tokens = lax.dynamic_index_in_dim(tokens, s, 0, keepdims=False)
    own_rows = jnp.concatenate([own_tokens, cotangent.reshape(2 * ROWS, D)], axis=0)
    own_rows = nn(own_rows, order).astype(BF)
    hidden_blocks = tensor_gather(own_rows[:ROWS])
    both_cotangents = own_rows[ROWS:]
    own_cotangent = lax.dynamic_slice_in_dim(both_cotangents, s * ROWS, ROWS, 0)
    grad_rows = lax.all_to_all(jnp.tile(both_cotangents, (4, 1)), "tensor", 0, 0, tiled=True)

    from_x = (ffn_straight, ffn_across, ffn_beside0)
    from_x, hidden_blocks, grad_rows, att_row0 = together(
        from_x, hidden_blocks, grad_rows, att_row0
    )
    ffn_straight, ffn_across, ffn_beside0 = from_x
    ffn_else = jnp.concatenate([ffn_straight, ffn_across], axis=0)
    ffn_pair0 = jnp.where(first, jnp.concatenate([ffn_own, ffn_beside0], axis=0), ffn_else)
    ffn_pair0, hidden_blocks = together(ffn_pair0, hidden_blocks)
    ffn_row0 = gather_row(ffn_pair0)
    grad_rows = grad_rows.reshape(4, 2, ROWS, D).swapaxes(0, 1).reshape(ROUTES, D)
    att_w = [(att_row0, swap_core(att_row0)), None]
    small = run(
        small_forward_kernel,
        [shaped((64, D), F32)],
        att_w[0],
        in_specs=[pl.BlockSpec((HALF, HD), lambda i: (0, ATT // HD))] * 2,
        out_specs=[pl.BlockSpec((64, D), lambda i: (0, 0))],
        grid=(1,),
    )[0]
    ffn_w = [None, None]
    kept = []
    for layer in (0, 1):
        at = 32 * layer
        attn_gain, ffn_gain = small[at : at + 1], small[at + 1 : at + 2]
        router = small[at + 2 : at + 2 + E].astype(BF)
        parts, att_saved = attention_forward(t_arg, hidden_blocks, attn_gain, att_w[layer])
        normed, *att_saved = att_saved
        mid, normed_ffn, copies = run(
            mid_kernel,
            [shaped((ROWS, D), F32), shaped((ROWS, D)), shaped((ROUTES, D))],
            [hidden_blocks[0], ffn_gain, parts[0], *tensor_send(parts)],
        )
        rows = group_exchange(copies)
        if layer == 0:
            normed, ffn_own = together(normed, ffn_own)
            ffn_beside1 = move(ffn_own, SIDE, lambda s, x: (s, x + 1), lambda s, x: s == 1)
            ffn_pair1 = jnp.where(first, ffn_else, jnp.concatenate([ffn_own, ffn_beside1], axis=0))
            ffn_row0, rows, att_pair1, ffn_pair1 = together(ffn_row0, rows, att_pair1, ffn_pair1)
            ffn_w[0] = (ffn_row0, swap_core(ffn_row0))
            att_row1 = gather_row(att_pair1)
            ffn_row1 = gather_row(ffn_pair1)
        else:
            ffn_row1, mid = together(ffn_row1, mid)
            ffn_w[1] = (ffn_row1, swap_core(ffn_row1))
        part, gates, own_gates, gate_up, gated = ffn_forward(
            s_arg, t_arg, rows, router, masks[layer], ffn_w[layer]
        )
        if layer == 1:
            sum1 = lax.psum_scatter(part, GROUP, scatter_dimension=0, tiled=True)
        kept.append((hidden_blocks[0], attn_gain, normed, *att_saved))
        kept.append((mid, ffn_gain, router, normed_ffn, rows, gates, own_gates, gate_up, gated))
        if layer == 0:
            outs = [shaped((ROWS, D))] * 2
            own_result, result = run(result_kernel, outs, [mid, group_exchange(part)])
            hidden_blocks = tensor_gather(own_result)
            att_row1, result = together(att_row1, result)
            att_w[1] = (att_row1, swap_core(att_row1))

    in_grads = [None, None]
    small_grads = [None, None]
    ffn_sums = [None, None]
    att_sums = [None, None]
    out_low = own_cotangent
    for layer in (1, 0):
        hidden, attn_gain, normed, qkv, probs, attended = kept[2 * layer]
        mid, ffn_gain, router, normed_ffn, rows, gates, own_gates, gate_up, gated = kept[2 * layer + 1]
        if layer == 0:
            gated, sum1 = together(gated, sum1)
        part_grad, gate_up_grad = ffn_backward(s_arg, grad_rows, gates, gate_up, ffn_w[layer])
        ffn_parts = (rows, grad_rows, gate_up_grad, gated)
        got = group_exchange(part_grad)
        own = ffn_weights(0, *ffn_parts, swap_core(ffn_weights(1, *ffn_parts)))
        got, own = together(got, own)
        if layer == 0:
            own, ffn_sums[1] = together(own, ffn_sums[1])
        ffn_sums[layer] = sum_row(own)
        mid_grad, mid_low, small = run(
            mid_backward_kernel,
            [shaped((ROWS, D), F32), shaped((ROWS, D)), shaped((SMALL, D), F32)],
            [mid, own_gates, out_low, ffn_gain, router, normed_ffn, got],
        )
        mid_blocks = tensor_gather(mid_low)
        parts, mid_rows, qkv_grad = attention_backward(mid_blocks, att_w[layer], qkv, probs)
        got = tensor_send(parts)
        att_parts = (normed, mid_rows, qkv_grad, attended)
        att_other = attention_weights(1, *att_parts)
        att_own = attention_weights(0, *att_parts, swap_core(att_other))
        if layer == 1:
            *got, att_other = together(*got, att_other)
        else:
            *got, att_own = together(*got, att_own)
        out_low, small_grads[layer], copies = run(
            hidden_backward_kernel,
            [shaped((ROWS, D)), shaped((SMALL, D), F32), shaped((ROUTES, D))],
            [hidden, attn_gain, mid_grad, small, parts[0], *got],
        )
        in_grads[layer] = out_low
        if layer == 1:
            grad_rows, att_own = together(group_exchange(copies), att_own)
            att_sums[1] = sum_row(att_own)
    def sum_z(part):
        blocks = rolled(part.reshape(4, 2 * DBLK, -1), z)
        total = blocks[0].astype(F32)
        for k in (1, 2, 3):
            total = total + move(blocks[k], ROW, lambda at, k=k: (at + k,)).astype(F32)
        return total.astype(BF)

    small_own, small_other = run(
        small_backward_kernel,
        [shaped((HALF, HD))] * 2,
        small_grads,
        scratch=[pltpu.VMEM((HD, D), F32)],
    )
    small_own = small_own.astype(F32) + swap_core(small_other).astype(F32)
    small_sum = sum_z(small_own.astype(BF))
    att_sums[0] = jnp.concatenate([sum_z(att_own), small_sum[:, :32]], axis=1)
    att_sums[1] = jnp.concatenate([att_sums[1], small_sum[:, 32:64]], axis=1)
    result1 = run(last_kernel, [shaped((ROWS, D))], [kept[3][0], sum1])[0]
    sums = [
        jnp.concatenate([ffn, att, jnp.zeros((2 * DBLK, HD - 32), BF)], axis=1)
        for ffn, att in zip(ffn_sums, att_sums)
    ]
    sums = together(*sums)

    same = jnp.where(first, sums[0], sums[1]).reshape(2, DBLK, -1)
    other = jnp.where(first, sums[1], sums[0]).reshape(2, DBLK, -1)
    beside = move(same[1], SIDE, lambda s, x: (s, x + 1))
    straight = move(other[0], SIDE, lambda s, x: (s + 1, x))
    across = move(other[1], SIDE, lambda s, x: (s + 1, x + 1))
    grads = run(
        final_kernel,
        [
            shaped(shape, F32)
            for shape in (
                (DBLK, GROUPS * HD),
                (DBLK, HD),
                (DBLK, HD),
                (DBLK, GROUPS * HD),
                (DBLK, 4 * HD),
                (DBLK, 2 * HD),
                (DBLK, 2 * E * HD),
                (E, DBLK, HD),
                (DBLK, HD),
            )
        ],
        [s_arg, same[0], beside, straight, across],
        1,
    )
    grad_query, grad_key, grad_value, grad_out, grad_shared_in, grad_shared_down = grads[:6]
    grad_expert_in, grad_expert_down, small = grads[6:]

    def both_sequences(values):
        low = nt(jnp.concatenate(values, axis=0), order).astype(BF).reshape(2, ROWS, D)
        mine = jnp.where(first, low[0], low[1])
        got = move(jnp.where(first, low[1], low[0]), SECTION, lambda s: (s + 1,))
        return jnp.where(first, jnp.stack([mine, got]), jnp.stack([got, mine]))[None]

    values_out = both_sequences([result, result1])
    grads_in = both_sequences(in_grads)

    small = rolled(small.reshape(4, DBLK // 4, HD), t)
    small_sum = small[0]
    for got in tensor_send([small[k] for k in range(4)]):
        small_sum = small_sum + got

    return (
        values_out,
        grads_in,
        small_sum[:, 0][None],
        grad_query[None],
        grad_key[None],
        grad_value[None],
        grad_out.T[None],
        small_sum[:, 1][None],
        small_sum[:, 2 : 2 + E][None],
        grad_shared_in.reshape(1, DBLK, 2, 2 * HD),
        grad_shared_down.T[None],
        grad_expert_in.reshape(1, DBLK, E, 2, HD),
        grad_expert_down.swapaxes(1, 2)[None],
    )


def solution(mesh):
    split = Mesh(
        mesh.devices.reshape(2, 2, 4, 2, 4), ("section", "xhi", "z", "core", "tensor")
    )
    dp = ("xhi", "z", "core")
    both = dp + ("tensor",)
    placed = (
        P(dp, "tensor", None),
        P(dp, "tensor", None),
        P("section", dp, None, None),
        P("section", dp, None, None),
        P("section", both),
        P("section", dp, "tensor"),
        P("section", dp, "tensor"),
        P("section", dp, "tensor"),
        P("section", "tensor", dp),
        P("section", both),
        P("section", both, None),
        P("section", dp, None, "tensor"),
        P("section", "tensor", dp),
        P("section", dp, None, None, "tensor"),
        P("section", None, "tensor", dp),
    )
    return jax.shard_map(
        per_device,
        mesh=split,
        in_specs=placed,
        out_specs=(
            P("section", dp, "tensor", None),
            P("section", dp, "tensor", None),
            P("section", both),
            P("section", dp, "tensor"),
            P("section", dp, "tensor"),
            P("section", dp, "tensor"),
            P("section", "tensor", dp),
            P("section", both),
            P("section", both, None),
            P("section", dp, None, "tensor"),
            P("section", "tensor", dp),
            P("section", dp, None, None, "tensor"),
            P("section", None, "tensor", dp),
        ),
        check_vma=False,
    )
```

```python
import jax
import jax.numpy as jnp
from jax import lax
from jax.experimental import pallas as pl
from jax.experimental.pallas import tpu as pltpu
from jax.sharding import Mesh
from jax.sharding import PartitionSpec as P

D = 1536
HD = 128
E = 16
HALF_E = 8
GROUPS = 3
LEN = 256
ROWS = 64
DBLK = 96
HALF = D // 2
ROUTES = 2 * LEN

NORM_EPSILON = 1e-05
MASK_VALUE = -1e30
SCALE = HD**-0.5

BF = jnp.bfloat16
F32 = jnp.float32

QKV = 640
ATT = 1024
ATT_PAD = 1152
BLOCKS = 9
STEPS = 3
STEP = 3 * HD
UP = BLOCKS * 256
DOWN = BLOCKS * 128
PIECE = UP + DOWN
WIDE = D + HD
SMALL = 24

SECTION = ("section",)
TENSOR = ("tensor",)
GROUP = ("section", "tensor")
CORE = ("core",)
ROW = ("z",)
SIDE = ("section", "xhi")


def dot(a, b, contract):
    return lax.dot_general(a, b, ((contract[:1], contract[1:]), ((), ())), preferred_element_type=F32)


def nn(a, b):
    return dot(a, b, (1, 0))


def nt(a, b):
    return dot(a, b, (1, 1))


def tn(a, b):
    return dot(a, b, (0, 0))


def move(block, axes, target, only=None):
    sizes = [lax.axis_size(axis) for axis in axes]
    pairs = []

    def flat(place):
        index = 0
        for size, at in zip(sizes, place):
            index = index * size + at % size
        return index

    def walk(place):
        if len(place) == len(sizes):
            if only is None or only(*place):
                pairs.append((flat(place), flat(target(*place))))
            return
        for at in range(sizes[len(place)]):
            walk(place + (at,))

    walk(())
    return lax.ppermute(block, axes, pairs)

SMEM = pl.BlockSpec(memory_space=pltpu.SMEM)


def shaped(shape, dtype=BF):
    return jax.ShapeDtypeStruct(shape, dtype)


def whole(array):
    return pl.BlockSpec(array.shape, lambda i: (0,) * array.ndim)


def run(
    kernel,
    outs,
    operands,
    scalars=0,
    flops=0,
    in_specs=None,
    out_specs=None,
    grid=(),
    scratch=(),
    far_in=(),
    far_out=(),
):
    if in_specs is None:
        in_specs = [SMEM] * scalars + [whole(x) for x in operands[scalars:]]
    if out_specs is None:
        grid = (1,)
        out_specs = [whole(x) for x in outs]
    limit = 28 if len(grid) and grid[0] == 3 else 12
    moved = sum(x.size * x.dtype.itemsize for x in list(operands) + list(outs))
    operands = [
        pltpu.with_memory_space_constraint(x, pltpu.HBM) if i in far_in else x
        for i, x in enumerate(operands)
    ]
    return pl.pallas_call(
        kernel,
        out_shape=[pltpu.HBM(x.shape, x.dtype) if i in far_out else x for i, x in enumerate(outs)],
        in_specs=in_specs,
        out_specs=out_specs,
        grid=grid,
        scratch_shapes=list(scratch),
        compiler_params=pltpu.CompilerParams(vmem_limit_bytes=limit * 1024 * 1024),
        cost_estimate=pl.CostEstimate(flops=flops, bytes_accessed=moved, transcendentals=0),
    )(*operands)


def together(*values):
    return lax.optimization_barrier(values)


def tensor_gather(rows):
    return [rows] + [move(rows, TENSOR, lambda t, k=k: (t - k,)) for k in (1, 2, 3)]


def tensor_send(parts):
    return [move(parts[k], TENSOR, lambda t, k=k: (t + k,)) for k in (1, 2, 3)]


def group_exchange(rows):
    return lax.all_to_all(rows, GROUP, 0, 0, tiled=True)


def rolled(stacked, shift):
    n = stacked.shape[0]
    return lax.dynamic_slice_in_dim(jnp.concatenate([stacked, stacked], axis=0), shift, n, 0)


def rms_factor(rows):
    return lax.rsqrt(jnp.mean(rows * rows, axis=-1, keepdims=True) + NORM_EPSILON)


def norm_backward(rows, gain, upstream):
    factor = rms_factor(rows)
    unit = rows * factor
    scaled = upstream * gain
    grad = factor * (scaled - unit * jnp.mean(scaled * unit, axis=-1, keepdims=True))
    return grad, jnp.sum(upstream * unit, axis=0, keepdims=True)


def add_up(refs):
    total = refs[0][...].astype(F32)
    for ref in refs[1:]:
        total = total + ref[...].astype(F32)
    return total


def block(index):
    return slice(index * ROWS, (index + 1) * ROWS)


def add_blocks(ref):
    total = ref[block(0), :].astype(F32)
    for index in range(1, 8):
        total = total + ref[block(index), :].astype(F32)
    return total


def head(index):
    return slice(index * HD, (index + 1) * HD)


KEYS = head(GROUPS)
VALUES = head(GROUPS + 1)


def attention_forward_kernel(t_ref, *refs):
    hidden, (gain, w0, w1) = refs[:4], refs[4:7]
    parts, (normed_ref, qkv_ref, probs_ref, attended_ref) = refs[7:11], refs[11:]
    for index, ref in enumerate(hidden):
        rows = ref[...].astype(F32)
        normed_ref[block(index), :] = (rows * rms_factor(rows) * gain[...]).astype(BF)
    normed = normed_ref[...]
    qkv = nn(normed[:, :HALF], w0[:, :QKV]) + nn(normed[:, HALF:], w1[:, :QKV])
    qkv = qkv.astype(BF)
    qkv_ref[...] = qkv

    def position(axis):
        return (t_ref[0] * ROWS + lax.broadcasted_iota(jnp.int32, (LEN, LEN), axis)) & (LEN - 1)

    causal = position(1) <= position(0)
    for g in range(GROUPS):
        scores = jnp.where(causal, nt(qkv[:, head(g)], qkv[:, KEYS]) * SCALE, MASK_VALUE)
        shifted = jnp.exp(scores - jnp.max(scores, axis=-1, keepdims=True))
        probs = (shifted / jnp.sum(shifted, axis=-1, keepdims=True)).astype(BF)
        probs_ref[g] = probs
        attended_ref[:, head(g)] = nn(probs, qkv[:, VALUES]).astype(BF)
    attended = attended_ref[...]
    for at, w in ((0, w0), (HALF, w1)):
        out = nt(attended, w[:, QKV:ATT]).astype(BF)
        for index, part in enumerate(parts):
            part[:, at : at + HALF] = out[block(index)]


def attention_forward(t, hidden_blocks, gain, weights):
    outs = [shaped((ROWS, D))] * 4
    outs += [shaped((LEN, D)), shaped((LEN, QKV)), shaped((GROUPS, LEN, LEN)), shaped((LEN, STEP))]
    flops = 2 * LEN * D * ATT + 4 * GROUPS * LEN * LEN * HD
    got = run(attention_forward_kernel, outs, [t, *hidden_blocks, gain, *weights], 1, flops, far_out=(4, 5, 6, 7))
    return got[:4], got[4:]


def attention_backward_kernel(*refs):
    grads, (w0, w1, qkv_ref, probs_ref) = refs[:4], refs[4:8]
    parts, (rows_ref, qkv_grad_ref) = refs[8:12], refs[12:]
    for index, ref in enumerate(grads):
        rows_ref[block(index), :] = ref[...]
    rows = rows_ref[...]
    attended_grad = nn(rows[:, :HALF], w0[:, QKV:ATT]) + nn(rows[:, HALF:], w1[:, QKV:ATT])
    attended_grad = attended_grad.astype(BF)
    qkv = qkv_ref[...]
    key_grad = jnp.zeros((LEN, HD), F32)
    value_grad = jnp.zeros((LEN, HD), F32)
    for g in range(GROUPS):
        probs = probs_ref[g]
        upstream = attended_grad[:, head(g)]
        value_grad = value_grad + tn(probs, upstream)
        prob_grad = nt(upstream, qkv[:, VALUES])
        wide = probs.astype(F32)
        score_grad = wide * (prob_grad - jnp.sum(wide * prob_grad, axis=-1, keepdims=True))
        score_grad = (score_grad * SCALE).astype(BF)
        qkv_grad_ref[:, head(g)] = nn(score_grad, qkv[:, KEYS]).astype(BF)
        key_grad = key_grad + tn(score_grad, qkv[:, head(g)])
    qkv_grad_ref[:, KEYS] = key_grad.astype(BF)
    qkv_grad_ref[:, VALUES] = value_grad.astype(BF)
    qkv_grad = qkv_grad_ref[...]
    for at, w in ((0, w0), (HALF, w1)):
        out = nt(qkv_grad, w[:, :QKV]).astype(BF)
        for index, part in enumerate(parts):
            part[:, at : at + HALF] = out[block(index)]


def attention_backward(grad_blocks, weights, qkv, probs):
    outs = [shaped((ROWS, D))] * 4 + [shaped((LEN, D)), shaped((LEN, QKV))]
    flops = 2 * LEN * D * ATT + 10 * GROUPS * LEN * LEN * HD
    got = run(attention_backward_kernel, outs, [*grad_blocks, *weights, qkv, probs], 0, flops, far_in=(6, 7))
    return got[:4], got[4], got[5]


def attention_weights_kernel(normed, rows, qkv_grad, attended, *refs):
    out = refs[-1]
    for columns, left, right in (
        (slice(0, QKV), normed, qkv_grad),
        (slice(QKV, ATT), rows, attended),
    ):
        total = tn(left[...], right[...])
        if len(refs) > 1:
            total = total + refs[0][:, columns].astype(F32)
        out[:, columns] = total.astype(BF)


def attention_weights(half, normed, rows, qkv_grad, attended, *other):
    def full(*shape):
        return pl.BlockSpec(shape, lambda i: (0, 0))

    cut = pl.BlockSpec((LEN, HALF), lambda i: (0, half))
    in_specs = [cut, cut, full(LEN, QKV), full(LEN, STEP)] + [full(HALF, ATT)] * len(other)
    return run(
        attention_weights_kernel,
        [shaped((HALF, ATT))],
        [normed, rows, qkv_grad, attended, *other],
        flops=2 * HALF * LEN * ATT,
        in_specs=in_specs,
        out_specs=[full(HALF, ATT)],
        grid=(1,),
    )[0]


def gate_column(gates, section, number):
    lane = lax.broadcasted_iota(jnp.int32, gates.shape, 1)
    picked = jnp.where(lane == section * HALF_E + number, gates, 0.0)
    return jnp.where(number == HALF_E, 1.0, jnp.sum(picked, axis=1, keepdims=True))


def ffn_forward_kernel(s_ref, t_ref, rows_ref, router, mask_ref, up0, up1, down0, down1, *refs):
    step = pl.program_id(0)
    part, gates_ref, own_ref, gate_up_ref, gated_ref, total = refs

    @pl.when(step == 0)
    def _():
        logits = nt(rows_ref[...], router[...])
        named = mask_ref[...] > 0.5
        top = jnp.max(jnp.where(named, logits, MASK_VALUE), axis=-1, keepdims=True)
        shifted = jnp.where(named, jnp.exp(jnp.where(named, logits - top, 0.0)), 0.0)
        gates_ref[...] = shifted / jnp.sum(shifted, axis=-1, keepdims=True)
        own_ref[...] = gates_ref[pl.ds((4 * s_ref[0] + t_ref[0]) * ROWS, ROWS), :]
        total[...] = jnp.zeros_like(total)

    gate_up = nn(rows_ref[:, :HALF], up0[...]) + nn(rows_ref[:, HALF:], up1[...])
    gate_up_ref[...] = gate_up.astype(BF)
    gates = gates_ref[...]
    for i in range(3):
        gate_part, up_part = gate_up[:, head(i)], gate_up[:, head(3 + i)]
        hidden = gate_part * jax.nn.sigmoid(gate_part) * up_part
        gated_ref[:, head(i)] = (hidden * gate_column(gates, s_ref[0], 3 * step + i)).astype(BF)
    gated = gated_ref[...]
    total[:, :HALF] += nt(gated, down0[...])
    total[:, HALF:] += nt(gated, down1[...])

    @pl.when(step == STEPS - 1)
    def _():
        part[...] = total[...].astype(BF)


def fixed(*shape):
    return pl.BlockSpec(shape, lambda j: (0,) * len(shape))


def by_step(rows, columns, first=0):
    return pl.BlockSpec((rows, columns), lambda j: (0, first + j))


def ffn_weight_specs():
    return [by_step(HALF, 2 * STEP)] * 2 + [by_step(HALF, STEP, UP // STEP)] * 2


def ffn_forward(s, t, rows, router, mask, weights):
    return run(
        ffn_forward_kernel,
        [
            shaped((ROUTES, D)),
            shaped((ROUTES, E), F32),
            shaped((ROWS, E), F32),
            shaped((ROUTES, UP)),
            shaped((ROUTES, DOWN)),
        ],
        [s, t, rows, router, mask, weights[0], weights[1], weights[0], weights[1]],
        flops=2 * ROUTES * D * PIECE,
        in_specs=[SMEM, SMEM, fixed(ROUTES, D), fixed(E, D), fixed(ROUTES, E)] + ffn_weight_specs(),
        out_specs=[fixed(ROUTES, D), fixed(ROUTES, E), fixed(ROWS, E)]
        + [by_step(ROUTES, 2 * STEP), by_step(ROUTES, STEP)],
        grid=(STEPS,),
        scratch=[pltpu.VMEM((ROUTES, D), F32)],
        far_out=(1, 2, 3, 4),
    )


def ffn_backward_kernel(s_ref, rows_ref, gates_ref, gate_up_ref, up0, up1, down0, down1, *refs):
    step = pl.program_id(0)
    part, grad_ref, total, products = refs

    @pl.when(step == 0)
    def _():
        total[...] = jnp.zeros_like(total)
        products[...] = jnp.zeros_like(products)

    hidden_grad = nn(rows_ref[:, :HALF], down0[...]) + nn(rows_ref[:, HALF:], down1[...])
    gates = gates_ref[...]
    lane = lax.broadcasted_iota(jnp.int32, (ROUTES, HD), 1)
    for i in range(3):
        number = 3 * step + i
        gate_part = gate_up_ref[:, head(i)].astype(F32)
        up_part = gate_up_ref[:, head(3 + i)].astype(F32)
        sigmoid = jax.nn.sigmoid(gate_part)
        silu = gate_part * sigmoid
        upstream = hidden_grad[:, head(i)]
        product = jnp.sum(silu * up_part * upstream, axis=1, keepdims=True)
        at = jnp.where(number < HALF_E, s_ref[0] * HALF_E + number, -1)
        products[...] = jnp.where(lane == at, product, products[...])
        upstream = upstream * gate_column(gates, s_ref[0], number)
        gate_grad = upstream * up_part * sigmoid * (1.0 + gate_part * (1.0 - sigmoid))
        grad_ref[:, head(i)] = gate_grad.astype(BF)
        grad_ref[:, head(3 + i)] = (upstream * silu).astype(BF)
    grad = grad_ref[...]
    total[:, :HALF] += nt(grad, up0[...])
    total[:, HALF:] += nt(grad, up1[...])

    @pl.when(step == STEPS - 1)
    def _():
        whole = products[...]
        high = whole.astype(BF).astype(F32)
        extra = high + pltpu.roll(whole - high, E, 1)
        part[:, :D] = total[...].astype(BF)
        part[:, D:] = extra.astype(BF)


def ffn_backward(s, rows, gates, gate_up, weights):
    return run(
        ffn_backward_kernel,
        [shaped((ROUTES, WIDE)), shaped((ROUTES, UP))],
        [s, rows, gates, gate_up, weights[0], weights[1], weights[0], weights[1]],
        flops=2 * ROUTES * D * PIECE,
        in_specs=[SMEM, fixed(ROUTES, D), fixed(ROUTES, E), by_step(ROUTES, 2 * STEP)]
        + ffn_weight_specs(),
        out_specs=[fixed(ROUTES, WIDE), by_step(ROUTES, 2 * STEP)],
        grid=(STEPS,),
        scratch=[pltpu.VMEM((ROUTES, D), F32), pltpu.VMEM((ROUTES, HD), F32)],
    )


def ffn_weights_kernel(rows, grad_rows, gate_up_grad, gated, *refs):
    step = pl.program_id(0)
    out = refs[-1]

    def store(total):
        if len(refs) > 1:
            total = total + refs[0][...].astype(F32)
        out[...] = total.astype(BF)

    @pl.when(step < 2)
    def _():
        store(tn(rows[...], gate_up_grad[...]))

    @pl.when(step == 2)
    def _():
        store(tn(grad_rows[...], gated[...]))


def ffn_weights(half, rows, grad_rows, gate_up_grad, gated, *other):
    cut = pl.BlockSpec((ROUTES, HALF), lambda j: (0, half))
    third = pl.BlockSpec((ROUTES, DOWN), lambda j: (0, jnp.minimum(j, 1)))
    return run(
        ffn_weights_kernel,
        [shaped((HALF, PIECE))],
        [rows, grad_rows, gate_up_grad, gated, *other],
        flops=2 * ROUTES * HALF * PIECE,
        in_specs=[cut, cut, third, fixed(ROUTES, DOWN)] + [by_step(HALF, DOWN)] * len(other),
        out_specs=[by_step(HALF, DOWN)],
        grid=(3,),
    )[0]


def mid_kernel(hidden, gain, *refs):
    mid_ref, normed_ref, copies = refs[-3:]
    mid = hidden[...].astype(F32) + add_up(refs[:-3])
    mid_ref[...] = mid
    normed = (mid * rms_factor(mid) * gain[...]).astype(BF)
    normed_ref[...] = normed
    for index in range(8):
        copies[block(index), :] = normed


def last_kernel(mid, total, out):
    out[...] = (mid[...] + total[...].astype(F32)).astype(BF)


def result_kernel(mid, got, *outs):
    result = (mid[...] + add_blocks(got)).astype(BF)
    for out in outs:
        out[...] = result


def mid_backward_kernel(mid, own_gates, out_grad, gain, router, normed, got, *refs):
    mid_grad_ref, low_ref, small = refs
    total = add_blocks(got)
    extra = total[:, D:]
    gate_grad = (extra + pltpu.roll(extra, HD - E, 1))[:, :E]
    own = own_gates[...]
    logits_grad = own * (gate_grad - jnp.sum(own * gate_grad, axis=1, keepdims=True))
    logits_grad = logits_grad.astype(BF)
    upstream = total[:, :D] + nn(logits_grad, router[...])
    small[...] = jnp.zeros_like(small)
    grad, small[1:2, :] = norm_backward(mid[...], gain[...], upstream)
    small[2 : 2 + E, :] = tn(logits_grad, normed[...])
    mid_grad = out_grad[...].astype(F32) + grad
    mid_grad_ref[...] = mid_grad
    low_ref[...] = mid_grad.astype(BF)


def hidden_backward_kernel(hidden, gain, mid_grad, small_in, *refs):
    out, small, copies = refs[-3:]
    small[...] = small_in[...]
    grad, small[0:1, :] = norm_backward(hidden[...].astype(F32), gain[...], add_up(refs[:-3]))
    low = (mid_grad[...] + grad).astype(BF)
    out[...] = low
    for index in range(8):
        copies[block(index), :] = low


def small_forward_kernel(own, other, out):
    out[:, :HALF] = own[...].astype(F32).T[:64]
    out[:, HALF:] = other[...].astype(F32).T[:64]


def small_backward_kernel(first, second, own, other, both):
    both[...] = jnp.zeros_like(both)
    both[:SMALL, :] = first[...]
    both[32 : 32 + SMALL, :] = second[...]
    own[...] = both[:, :HALF].T.astype(BF)
    other[...] = both[:, HALF:].T.astype(BF)


def pack_kernel(s_ref, ffn0, ffn1, att1, *refs):
    outs = refs[4:]
    total = add_up(refs[:4])
    att0, small = total[:, :ATT].astype(BF), total[:, ATT:]
    smalls = (small.astype(BF), pltpu.roll(small, HD - 32, 1).astype(BF))
    for layer, ffn, att in ((0, ffn0, att0), (1, ffn1, att1[...])):
        for index in (0, 1):
            cut = slice(index * DBLK, (index + 1) * DBLK)
            for mine in (0, 1):

                @pl.when((s_ref[0] == layer) == (mine == 0))
                def _(out=outs[2 * mine + index]):
                    out[:, :PIECE] = ffn[cut, :]
                    out[:, PIECE : PIECE + ATT] = att[cut]
                    out[:, PIECE + ATT :] = smalls[layer][cut]


def final_kernel(s_ref, own, beside, straight, across, *outs):
    query, key, value, out, shared_in, shared_down, expert_in, expert_down, small = outs
    mine = own[...].astype(F32) + beside[...].astype(F32)
    theirs = straight[...].astype(F32) + across[...].astype(F32)
    att = mine[:, PIECE:] + theirs[:, PIECE:]
    query[...] = att[:, : GROUPS * HD]
    key[...] = att[:, KEYS]
    value[...] = att[:, VALUES]
    out[...] = att[:, QKV:ATT]
    small[...] = att[:, ATT:]
    for half in (0, 1):
        part = jnp.where(s_ref[0] == half, mine, theirs)
        for number in range(BLOCKS):
            at = number // 3 * 2 * STEP + number % 3 * HD
            gate_part, up_part = part[:, at : at + HD], part[:, at + STEP : at + STEP + HD]
            down = part[:, UP + number * HD : UP + (number + 1) * HD]
            if number < HALF_E:
                expert = half * HALF_E + number
                expert_in[:, head(2 * expert)] = gate_part
                expert_in[:, head(2 * expert + 1)] = up_part
                expert_down[expert] = down
            else:
                shared_in[:, head(half)] = gate_part
                shared_in[:, head(2 + half)] = up_part
                shared_down[:, head(half)] = down


def swap_core(part):
    return move(part, CORE, lambda c: (1 - c,))


def sum_row(part):
    return lax.psum_scatter(part, "z", scatter_dimension=0, tiled=True)


def gather_row(part):
    return lax.all_gather(part, "z", axis=0, tiled=True)


def per_device(
    tokens,
    cotangent,
    route_experts,
    route_slots,
    gain_attn,
    w_query,
    w_key,
    w_value,
    w_out,
    gain_ffn,
    w_router,
    w_shared_in,
    w_shared_down,
    w_expert_in,
    w_expert_down,
):
    s = lax.axis_index("section")
    xhi = lax.axis_index("xhi")
    core = lax.axis_index("core")
    z = lax.axis_index("z")
    t = lax.axis_index("tensor")
    first = s == 0
    s_arg = s.astype(jnp.int32)[None]
    t_arg = t.astype(jnp.int32)[None]

    small = jnp.concatenate([gain_attn[0][:, None], gain_ffn[0][:, None], w_router[0]], axis=1)
    small = jnp.pad(small, ((0, 0), (0, HD - 2 - E)))
    small = rolled(jnp.stack(tensor_gather(small)), (4 - t) % 4).reshape(DBLK, HD)
    att_piece = jnp.concatenate([w_query[0], w_key[0], w_value[0], w_out[0].T], axis=1)

    expert_in = w_expert_in[0].reshape(DBLK, 2, HALF_E, 2, HD)
    shared_in = w_shared_in[0].reshape(DBLK, 2, 2, HD)
    expert_down = w_expert_down[0].transpose(2, 0, 1).reshape(DBLK, 2, HALF_E * HD)
    shared_down = w_shared_down[0].T.reshape(DBLK, 2, HD)

    def ffn_piece(part):
        up = jnp.concatenate([expert_in[:, part], shared_in[:, None, :, part]], axis=1)
        up = up.reshape(DBLK, STEPS, 3, 2, HD).swapaxes(2, 3).reshape(DBLK, UP)
        return jnp.concatenate([up, expert_down[:, part], shared_down[:, part]], axis=1)

    ffn_own = jnp.where(first, ffn_piece(0), ffn_piece(1))
    ffn_other = jnp.where(first, ffn_piece(1), ffn_piece(0))

    place = jnp.arange(D, dtype=jnp.int32)
    at_core = (place // HALF + core) % 2
    at_z = (place // (2 * DBLK)) % 4
    at_x = (place // DBLK + xhi) % 2
    column = at_x * HALF + at_z * (2 * DBLK) + at_core * DBLK + place % DBLK
    order = (place[:, None] == column[None, :]).astype(BF)

    own_tokens = lax.dynamic_index_in_dim(tokens, s, 0, keepdims=False)
    own_rows = nn(own_tokens, order).astype(BF)
    grad_rows = lax.all_gather(cotangent.reshape(2 * ROWS, D), "tensor", axis=0, tiled=True)

    named = jnp.sum((route_experts[0][:, :, :, None] == jnp.arange(E)).astype(F32), axis=2)
    named = named.astype(BF).reshape(ROUTES, E)
    named_else = move(named, SECTION, lambda s: (s + 1,))
    small, named_else, own_rows = together(small, named_else, own_rows)
    masks = [jnp.where(s == layer, named, named_else).astype(F32) for layer in (0, 1)]

    att_beside = move(att_piece, SIDE, lambda s, x: (s, x + 1))
    att_straight = move(att_piece, SIDE, lambda s, x: (s + 1, x))
    att_across = move(att_piece, SIDE, lambda s, x: (s + 1, x + 1))
    small_x = [
        small,
        move(small, SIDE, lambda s, x: (s, x + 1)),
        move(small, SIDE, lambda s, x: (s + 1, x)),
        move(small, SIDE, lambda s, x: (s + 1, x + 1)),
    ]
    att_straight, small_x, ffn_own, ffn_other = together(att_straight, small_x, ffn_own, ffn_other)
    att_same = jnp.concatenate([att_piece, att_beside], axis=0)
    att_else = jnp.concatenate([att_straight, att_across], axis=0)
    att_pairs = [jnp.where(first, att_same, att_else), jnp.where(first, att_else, att_same)]
    ffn_straight = move(ffn_other, SIDE, lambda s, x: (s + 1, x))
    ffn_across = move(ffn_other, SIDE, lambda s, x: (s + 1, x + 1))
    ffn_beside0 = move(ffn_own, SIDE, lambda s, x: (s, x + 1), lambda s, x: s == 0)

    small_same = jnp.concatenate(small_x[:2], axis=0)[:, :32]
    small_else = jnp.concatenate(small_x[2:], axis=0)[:, :32]
    att_pair0 = jnp.concatenate(
        [
            att_pairs[0],
            jnp.where(first, small_same, small_else),
            jnp.where(first, small_else, small_same),
            jnp.zeros((2 * DBLK, HD - 64), BF),
        ],
        axis=1,
    )
    att_pair1 = att_pairs[1]
    att_pair0, grad_rows = together(att_pair0, grad_rows)
    att_row0 = gather_row(att_pair0)

    hidden_blocks = tensor_gather(own_rows)
    grad_rows = nn(grad_rows, order).astype(BF)
    grad_rows = grad_rows.reshape(4, 2, ROWS, D).swapaxes(0, 1).reshape(ROUTES, D)
    own_cotangent = lax.dynamic_slice_in_dim(grad_rows, (4 * s + t) * ROWS, ROWS, 0)

    from_x = (ffn_straight, ffn_across, ffn_beside0)
    from_x, hidden_blocks, att_row0 = together(from_x, hidden_blocks, att_row0)
    ffn_straight, ffn_across, ffn_beside0 = from_x
    ffn_else = jnp.concatenate([ffn_straight, ffn_across], axis=0)
    ffn_pair0 = jnp.where(first, jnp.concatenate([ffn_own, ffn_beside0], axis=0), ffn_else)
    ffn_pair0, hidden_blocks = together(ffn_pair0, hidden_blocks)
    ffn_row0 = gather_row(ffn_pair0)
    att_w = [(att_row0, swap_core(att_row0)), None]
    small = run(
        small_forward_kernel,
        [shaped((64, D), F32)],
        att_w[0],
        in_specs=[pl.BlockSpec((HALF, HD), lambda i: (0, ATT // HD))] * 2,
        out_specs=[pl.BlockSpec((64, D), lambda i: (0, 0))],
        grid=(1,),
    )[0]
    ffn_w = [None, None]
    kept = []
    for layer in (0, 1):
        at = 32 * layer
        attn_gain, ffn_gain = small[at : at + 1], small[at + 1 : at + 2]
        router = small[at + 2 : at + 2 + E].astype(BF)
        parts, att_saved = attention_forward(t_arg, hidden_blocks, attn_gain, att_w[layer])
        normed, *att_saved = att_saved
        mid, normed_ffn, copies = run(
            mid_kernel,
            [shaped((ROWS, D), F32), shaped((ROWS, D)), shaped((ROUTES, D))],
            [hidden_blocks[0], ffn_gain, parts[0], *tensor_send(parts)],
            far_out=(1,),
        )
        rows = group_exchange(copies)
        if layer == 0:
            normed, ffn_own = together(normed, ffn_own)
            ffn_beside1 = move(ffn_own, SIDE, lambda s, x: (s, x + 1), lambda s, x: s == 1)
            ffn_pair1 = jnp.where(first, ffn_else, jnp.concatenate([ffn_own, ffn_beside1], axis=0))
            ffn_row0, rows, att_pair1, ffn_pair1 = together(ffn_row0, rows, att_pair1, ffn_pair1)
            ffn_w[0] = (ffn_row0, swap_core(ffn_row0))
            att_row1 = gather_row(att_pair1)
            ffn_row1 = gather_row(ffn_pair1)
        else:
            ffn_row1, mid = together(ffn_row1, mid)
            ffn_w[1] = (ffn_row1, swap_core(ffn_row1))
        part, gates, own_gates, gate_up, gated = ffn_forward(
            s_arg, t_arg, rows, router, masks[layer], ffn_w[layer]
        )
        if layer == 1:
            sum1 = lax.psum_scatter(part, GROUP, scatter_dimension=0, tiled=True)
        kept.append((hidden_blocks[0], attn_gain, normed, *att_saved))
        kept.append((mid, ffn_gain, router, normed_ffn, rows, gates, own_gates, gate_up, gated))
        if layer == 0:
            outs = [shaped((ROWS, D))] * 2
            own_result, result = run(result_kernel, outs, [mid, group_exchange(part)])
            hidden_blocks = tensor_gather(own_result)
            att_row1, result = together(att_row1, result)
            att_w[1] = (att_row1, swap_core(att_row1))

    in_grads = [None, None]
    small_grads = [None, None]
    ffn_sums = [None, None]
    att_sums = [None, None]
    out_low = own_cotangent
    for layer in (1, 0):
        hidden, attn_gain, normed, qkv, probs, attended = kept[2 * layer]
        mid, ffn_gain, router, normed_ffn, rows, gates, own_gates, gate_up, gated = kept[2 * layer + 1]
        if layer == 0:
            gated, sum1 = together(gated, sum1)
        part_grad, gate_up_grad = ffn_backward(s_arg, grad_rows, gates, gate_up, ffn_w[layer])
        ffn_parts = (rows, grad_rows, gate_up_grad, gated)
        got = group_exchange(part_grad)
        own = ffn_weights(0, *ffn_parts, swap_core(ffn_weights(1, *ffn_parts)))
        got, own = together(got, own)
        if layer == 0:
            own, ffn_sums[1] = together(own, ffn_sums[1])
        ffn_sums[layer] = sum_row(own)
        mid_grad, mid_low, small = run(
            mid_backward_kernel,
            [shaped((ROWS, D), F32), shaped((ROWS, D)), shaped((SMALL, D), F32)],
            [mid, own_gates, out_low, ffn_gain, router, normed_ffn, got],
            far_in=(0, 1, 2, 3, 4, 5),
            far_out=(0, 2),
        )
        mid_blocks = tensor_gather(mid_low)
        parts, mid_rows, qkv_grad = attention_backward(mid_blocks, att_w[layer], qkv, probs)
        got = tensor_send(parts)
        att_parts = (normed, mid_rows, qkv_grad, attended)
        att_other = attention_weights(1, *att_parts)
        att_own = attention_weights(0, *att_parts, swap_core(att_other))
        if layer == 1:
            *got, att_other = together(*got, att_other)
        else:
            *got, att_own = together(*got, att_own)
        out_low, small_grads[layer], copies = run(
            hidden_backward_kernel,
            [shaped((ROWS, D)), shaped((SMALL, D), F32), shaped((ROUTES, D))],
            [hidden, attn_gain, mid_grad, small, parts[0], *got],
            far_in=(0, 1, 2, 3),
            far_out=(0, 1),
        )
        in_grads[layer] = out_low
        if layer == 1:
            grad_rows, att_own = together(group_exchange(copies), att_own)
            att_sums[1] = sum_row(att_own)
    def spread_z(part):
        blocks = rolled(part.reshape(4, 2 * DBLK, -1), z)
        return [blocks[0]] + [move(blocks[k], ROW, lambda at, k=k: (at + k,)) for k in (1, 2, 3)]

    small_own, small_other = run(
        small_backward_kernel,
        [shaped((HALF, HD))] * 2,
        small_grads,
        scratch=[pltpu.VMEM((HD, D), F32)],
    )
    small_own = (small_own.astype(F32) + swap_core(small_other).astype(F32)).astype(BF)
    att_blocks = spread_z(jnp.concatenate([att_own, small_own], axis=1))
    result1 = run(last_kernel, [shaped((ROWS, D))], [kept[3][0], sum1])[0]

    same0, same1, other0, other1 = run(
        pack_kernel,
        [shaped((DBLK, PIECE + ATT_PAD))] * 4,
        [s_arg, *ffn_sums, att_sums[1], *att_blocks],
        1,
    )
    beside = move(same1, SIDE, lambda s, x: (s, x + 1))
    straight = move(other0, SIDE, lambda s, x: (s + 1, x))
    across = move(other1, SIDE, lambda s, x: (s + 1, x + 1))
    grads = run(
        final_kernel,
        [
            shaped(shape, F32)
            for shape in (
                (DBLK, GROUPS * HD),
                (DBLK, HD),
                (DBLK, HD),
                (DBLK, GROUPS * HD),
                (DBLK, 4 * HD),
                (DBLK, 2 * HD),
                (DBLK, 2 * E * HD),
                (E, DBLK, HD),
                (DBLK, HD),
            )
        ],
        [s_arg, same0, beside, straight, across],
        1,
    )
    grad_query, grad_key, grad_value, grad_out, grad_shared_in, grad_shared_down = grads[:6]
    grad_expert_in, grad_expert_down, small = grads[6:]

    def both_sequences(values):
        low = nt(jnp.concatenate(values, axis=0), order).astype(BF).reshape(2, ROWS, D)
        mine = jnp.where(first, low[0], low[1])
        got = move(jnp.where(first, low[1], low[0]), SECTION, lambda s: (s + 1,))
        return jnp.where(first, jnp.stack([mine, got]), jnp.stack([got, mine]))[None]

    values_out = both_sequences([result, result1])
    grads_in = both_sequences(in_grads)

    small = rolled(small.reshape(4, DBLK // 4, HD), t)
    small_sum = small[0]
    for got in tensor_send([small[k] for k in range(4)]):
        small_sum = small_sum + got

    return (
        values_out,
        grads_in,
        small_sum[:, 0][None],
        grad_query[None],
        grad_key[None],
        grad_value[None],
        grad_out.T[None],
        small_sum[:, 1][None],
        small_sum[:, 2 : 2 + E][None],
        grad_shared_in.reshape(1, DBLK, 2, 2 * HD),
        grad_shared_down.T[None],
        grad_expert_in.reshape(1, DBLK, E, 2, HD),
        grad_expert_down.swapaxes(1, 2)[None],
    )


def solution(mesh):
    split = Mesh(
        mesh.devices.reshape(2, 2, 4, 2, 4), ("section", "xhi", "z", "core", "tensor")
    )
    dp = ("xhi", "z", "core")
    both = dp + ("tensor",)
    placed = (
        P(dp, "tensor", None),
        P(dp, "tensor", None),
        P("section", dp, None, None),
        P("section", dp, None, None),
        P("section", both),
        P("section", dp, "tensor"),
        P("section", dp, "tensor"),
        P("section", dp, "tensor"),
        P("section", "tensor", dp),
        P("section", both),
        P("section", both, None),
        P("section", dp, None, "tensor"),
        P("section", "tensor", dp),
        P("section", dp, None, None, "tensor"),
        P("section", None, "tensor", dp),
    )
    return jax.shard_map(
        per_device,
        mesh=split,
        in_specs=placed,
        out_specs=(
            P("section", dp, "tensor", None),
            P("section", dp, "tensor", None),
            P("section", both),
            P("section", dp, "tensor"),
            P("section", dp, "tensor"),
            P("section", dp, "tensor"),
            P("section", "tensor", dp),
            P("section", both),
            P("section", both, None),
            P("section", dp, None, "tensor"),
            P("section", "tensor", dp),
            P("section", dp, None, None, "tensor"),
            P("section", None, "tensor", dp),
        ),
        check_vma=False,
    )
```

```python
import jax
import jax.numpy as jnp
from jax import lax
from jax.experimental import pallas as pl
from jax.experimental.pallas import tpu as pltpu
from jax.sharding import Mesh
from jax.sharding import PartitionSpec as P

D = 1536
HD = 128
E = 16
HALF_E = 8
GROUPS = 3
LEN = 256
ROWS = 64
DBLK = 96
HALF = D // 2
ROUTES = 2 * LEN

NORM_EPSILON = 1e-05
MASK_VALUE = -1e30
SCALE = HD**-0.5

BF = jnp.bfloat16
F32 = jnp.float32

QKV = 640
ATT = 1024
ATT_PAD = 1152
BLOCKS = 9
STEPS = 3
STEP = 3 * HD
UP = BLOCKS * 256
DOWN = BLOCKS * 128
PIECE = UP + DOWN
WIDE = D + HD
SMALL = 24

SECTION = ("section",)
TENSOR = ("tensor",)
GROUP = ("section", "tensor")
CORE = ("core",)
ROW = ("z",)
SIDE = ("section", "xhi")


def dot(a, b, contract):
    return lax.dot_general(a, b, ((contract[:1], contract[1:]), ((), ())), preferred_element_type=F32)


def nn(a, b):
    return dot(a, b, (1, 0))


def nt(a, b):
    return dot(a, b, (1, 1))


def tn(a, b):
    return dot(a, b, (0, 0))


def move(block, axes, target, only=None):
    sizes = [lax.axis_size(axis) for axis in axes]
    pairs = []

    def flat(place):
        index = 0
        for size, at in zip(sizes, place):
            index = index * size + at % size
        return index

    def walk(place):
        if len(place) == len(sizes):
            if only is None or only(*place):
                pairs.append((flat(place), flat(target(*place))))
            return
        for at in range(sizes[len(place)]):
            walk(place + (at,))

    walk(())
    return lax.ppermute(block, axes, pairs)

SMEM = pl.BlockSpec(memory_space=pltpu.SMEM)


def shaped(shape, dtype=BF):
    return jax.ShapeDtypeStruct(shape, dtype)


def whole(array):
    return pl.BlockSpec(array.shape, lambda i: (0,) * array.ndim)


def run(
    kernel,
    outs,
    operands,
    scalars=0,
    flops=0,
    in_specs=None,
    out_specs=None,
    grid=(),
    scratch=(),
    far_in=(),
    far_out=(),
):
    if in_specs is None:
        in_specs = [SMEM] * scalars + [whole(x) for x in operands[scalars:]]
    if out_specs is None:
        grid = (1,)
        out_specs = [whole(x) for x in outs]
    limit = 28 if len(grid) and grid[0] == 3 else 12
    moved = sum(x.size * x.dtype.itemsize for x in list(operands) + list(outs))
    operands = [
        pltpu.with_memory_space_constraint(x, pltpu.HBM) if i in far_in else x
        for i, x in enumerate(operands)
    ]
    return pl.pallas_call(
        kernel,
        out_shape=[pltpu.HBM(x.shape, x.dtype) if i in far_out else x for i, x in enumerate(outs)],
        in_specs=in_specs,
        out_specs=out_specs,
        grid=grid,
        scratch_shapes=list(scratch),
        compiler_params=pltpu.CompilerParams(vmem_limit_bytes=limit * 1024 * 1024),
        cost_estimate=pl.CostEstimate(flops=flops, bytes_accessed=moved, transcendentals=0),
    )(*operands)


def together(*values):
    return lax.optimization_barrier(values)


def tensor_gather(rows):
    return [rows] + [move(rows, TENSOR, lambda t, k=k: (t - k,)) for k in (1, 2, 3)]


def tensor_send(parts):
    return [move(parts[k], TENSOR, lambda t, k=k: (t + k,)) for k in (1, 2, 3)]


def group_exchange(rows):
    return lax.all_to_all(rows, GROUP, 0, 0, tiled=True)


def rolled(stacked, shift):
    n = stacked.shape[0]
    return lax.dynamic_slice_in_dim(jnp.concatenate([stacked, stacked], axis=0), shift, n, 0)


def rms_factor(rows):
    return lax.rsqrt(jnp.mean(rows * rows, axis=-1, keepdims=True) + NORM_EPSILON)


def norm_backward(rows, gain, upstream):
    factor = rms_factor(rows)
    unit = rows * factor
    scaled = upstream * gain
    grad = factor * (scaled - unit * jnp.mean(scaled * unit, axis=-1, keepdims=True))
    return grad, jnp.sum(upstream * unit, axis=0, keepdims=True)


def add_up(refs):
    total = refs[0][...].astype(F32)
    for ref in refs[1:]:
        total = total + ref[...].astype(F32)
    return total


def block(index):
    return slice(index * ROWS, (index + 1) * ROWS)


def add_blocks(ref):
    total = ref[block(0), :].astype(F32)
    for index in range(1, 8):
        total = total + ref[block(index), :].astype(F32)
    return total


def head(index):
    return slice(index * HD, (index + 1) * HD)


KEYS = head(GROUPS)
VALUES = head(GROUPS + 1)


def attention_forward_kernel(t_ref, *refs):
    hidden, (gain, w0, w1) = refs[:4], refs[4:7]
    parts, (normed_ref, qkv_ref, probs_ref, attended_ref) = refs[7:11], refs[11:]
    for index, ref in enumerate(hidden):
        rows = ref[...].astype(F32)
        normed_ref[block(index), :] = (rows * rms_factor(rows) * gain[...]).astype(BF)
    normed = normed_ref[...]
    qkv = nn(normed[:, :HALF], w0[:, :QKV]) + nn(normed[:, HALF:], w1[:, :QKV])
    qkv = qkv.astype(BF)
    qkv_ref[...] = qkv

    def position(axis):
        return (t_ref[0] * ROWS + lax.broadcasted_iota(jnp.int32, (LEN, LEN), axis)) & (LEN - 1)

    causal = position(1) <= position(0)
    for g in range(GROUPS):
        scores = jnp.where(causal, nt(qkv[:, head(g)], qkv[:, KEYS]) * SCALE, MASK_VALUE)
        shifted = jnp.exp(scores - jnp.max(scores, axis=-1, keepdims=True))
        probs = (shifted / jnp.sum(shifted, axis=-1, keepdims=True)).astype(BF)
        probs_ref[g] = probs
        attended_ref[:, head(g)] = nn(probs, qkv[:, VALUES]).astype(BF)
    attended = attended_ref[...]
    for at, w in ((0, w0), (HALF, w1)):
        out = nt(attended, w[:, QKV:ATT]).astype(BF)
        for index, part in enumerate(parts):
            part[:, at : at + HALF] = out[block(index)]


def attention_forward(t, hidden_blocks, gain, weights):
    outs = [shaped((ROWS, D))] * 4
    outs += [shaped((LEN, D)), shaped((LEN, QKV)), shaped((GROUPS, LEN, LEN)), shaped((LEN, STEP))]
    flops = 2 * LEN * D * ATT + 4 * GROUPS * LEN * LEN * HD
    got = run(attention_forward_kernel, outs, [t, *hidden_blocks, gain, *weights], 1, flops, far_out=(4, 5, 6, 7))
    return got[:4], got[4:]


def attention_backward_kernel(*refs):
    grads, (w0, w1, qkv_ref, probs_ref) = refs[:4], refs[4:8]
    parts, (rows_ref, qkv_grad_ref) = refs[8:12], refs[12:]
    for index, ref in enumerate(grads):
        rows_ref[block(index), :] = ref[...]
    rows = rows_ref[...]
    attended_grad = nn(rows[:, :HALF], w0[:, QKV:ATT]) + nn(rows[:, HALF:], w1[:, QKV:ATT])
    attended_grad = attended_grad.astype(BF)
    qkv = qkv_ref[...]
    key_grad = jnp.zeros((LEN, HD), F32)
    value_grad = jnp.zeros((LEN, HD), F32)
    for g in range(GROUPS):
        probs = probs_ref[g]
        upstream = attended_grad[:, head(g)]
        value_grad = value_grad + tn(probs, upstream)
        prob_grad = nt(upstream, qkv[:, VALUES])
        wide = probs.astype(F32)
        score_grad = wide * (prob_grad - jnp.sum(wide * prob_grad, axis=-1, keepdims=True))
        score_grad = (score_grad * SCALE).astype(BF)
        qkv_grad_ref[:, head(g)] = nn(score_grad, qkv[:, KEYS]).astype(BF)
        key_grad = key_grad + tn(score_grad, qkv[:, head(g)])
    qkv_grad_ref[:, KEYS] = key_grad.astype(BF)
    qkv_grad_ref[:, VALUES] = value_grad.astype(BF)
    qkv_grad = qkv_grad_ref[...]
    for at, w in ((0, w0), (HALF, w1)):
        out = nt(qkv_grad, w[:, :QKV]).astype(BF)
        for index, part in enumerate(parts):
            part[:, at : at + HALF] = out[block(index)]


def attention_backward(grad_blocks, weights, qkv, probs):
    outs = [shaped((ROWS, D))] * 4 + [shaped((LEN, D)), shaped((LEN, QKV))]
    flops = 2 * LEN * D * ATT + 10 * GROUPS * LEN * LEN * HD
    got = run(attention_backward_kernel, outs, [*grad_blocks, *weights, qkv, probs], 0, flops, far_in=(6, 7))
    return got[:4], got[4], got[5]


def attention_weights_kernel(normed, rows, qkv_grad, attended, *refs):
    out = refs[-1]
    for columns, left, right in (
        (slice(0, QKV), normed, qkv_grad),
        (slice(QKV, ATT), rows, attended),
    ):
        total = tn(left[...], right[...])
        if len(refs) > 1:
            total = total + refs[0][:, columns].astype(F32)
        out[:, columns] = total.astype(BF)


def attention_weights(half, normed, rows, qkv_grad, attended, *other):
    def full(*shape):
        return pl.BlockSpec(shape, lambda i: (0, 0))

    cut = pl.BlockSpec((LEN, HALF), lambda i: (0, half))
    in_specs = [cut, cut, full(LEN, QKV), full(LEN, STEP)] + [full(HALF, ATT)] * len(other)
    return run(
        attention_weights_kernel,
        [shaped((HALF, ATT))],
        [normed, rows, qkv_grad, attended, *other],
        flops=2 * HALF * LEN * ATT,
        in_specs=in_specs,
        out_specs=[full(HALF, ATT)],
        grid=(1,),
    )[0]


def gate_column(gates, section, number):
    lane = lax.broadcasted_iota(jnp.int32, gates.shape, 1)
    picked = jnp.where(lane == section * HALF_E + number, gates, 0.0)
    return jnp.where(number == HALF_E, 1.0, jnp.sum(picked, axis=1, keepdims=True))


def ffn_forward_kernel(s_ref, t_ref, rows_ref, router, mask_ref, up0, up1, down0, down1, *refs):
    step = pl.program_id(0)
    part, gates_ref, own_ref, gate_up_ref, gated_ref, total = refs

    @pl.when(step == 0)
    def _():
        logits = nt(rows_ref[...], router[...])
        named = mask_ref[...] > 0.5
        top = jnp.max(jnp.where(named, logits, MASK_VALUE), axis=-1, keepdims=True)
        shifted = jnp.where(named, jnp.exp(jnp.where(named, logits - top, 0.0)), 0.0)
        gates_ref[...] = shifted / jnp.sum(shifted, axis=-1, keepdims=True)
        own_ref[...] = gates_ref[pl.ds((4 * s_ref[0] + t_ref[0]) * ROWS, ROWS), :]
        total[...] = jnp.zeros_like(total)

    gate_up = nn(rows_ref[:, :HALF], up0[...]) + nn(rows_ref[:, HALF:], up1[...])
    gate_up_ref[...] = gate_up.astype(BF)
    gates = gates_ref[...]
    for i in range(3):
        gate_part, up_part = gate_up[:, head(i)], gate_up[:, head(3 + i)]
        hidden = gate_part * jax.nn.sigmoid(gate_part) * up_part
        gated_ref[:, head(i)] = (hidden * gate_column(gates, s_ref[0], 3 * step + i)).astype(BF)
    gated = gated_ref[...]
    total[:, :HALF] += nt(gated, down0[...])
    total[:, HALF:] += nt(gated, down1[...])

    @pl.when(step == STEPS - 1)
    def _():
        part[...] = total[...].astype(BF)


def fixed(*shape):
    return pl.BlockSpec(shape, lambda j: (0,) * len(shape))


def by_step(rows, columns, first=0):
    return pl.BlockSpec((rows, columns), lambda j: (0, first + j))


def ffn_weight_specs():
    return [by_step(HALF, 2 * STEP)] * 2 + [by_step(HALF, STEP, UP // STEP)] * 2


def ffn_forward(s, t, rows, router, mask, weights):
    return run(
        ffn_forward_kernel,
        [
            shaped((ROUTES, D)),
            shaped((ROUTES, E), F32),
            shaped((ROWS, E), F32),
            shaped((ROUTES, UP)),
            shaped((ROUTES, DOWN)),
        ],
        [s, t, rows, router, mask, weights[0], weights[1], weights[0], weights[1]],
        flops=2 * ROUTES * D * PIECE,
        in_specs=[SMEM, SMEM, fixed(ROUTES, D), fixed(E, D), fixed(ROUTES, E)] + ffn_weight_specs(),
        out_specs=[fixed(ROUTES, D), fixed(ROUTES, E), fixed(ROWS, E)]
        + [by_step(ROUTES, 2 * STEP), by_step(ROUTES, STEP)],
        grid=(STEPS,),
        scratch=[pltpu.VMEM((ROUTES, D), F32)],
        far_in=(5, 6, 7, 8),
        far_out=(1, 2, 3, 4),
    )


def ffn_backward_kernel(s_ref, rows_ref, gates_ref, gate_up_ref, up0, up1, down0, down1, *refs):
    step = pl.program_id(0)
    part, grad_ref, total, products = refs

    @pl.when(step == 0)
    def _():
        total[...] = jnp.zeros_like(total)
        products[...] = jnp.zeros_like(products)

    hidden_grad = nn(rows_ref[:, :HALF], down0[...]) + nn(rows_ref[:, HALF:], down1[...])
    gates = gates_ref[...]
    lane = lax.broadcasted_iota(jnp.int32, (ROUTES, HD), 1)
    for i in range(3):
        number = 3 * step + i
        gate_part = gate_up_ref[:, head(i)].astype(F32)
        up_part = gate_up_ref[:, head(3 + i)].astype(F32)
        sigmoid = jax.nn.sigmoid(gate_part)
        silu = gate_part * sigmoid
        upstream = hidden_grad[:, head(i)]
        product = jnp.sum(silu * up_part * upstream, axis=1, keepdims=True)
        at = jnp.where(number < HALF_E, s_ref[0] * HALF_E + number, -1)
        products[...] = jnp.where(lane == at, product, products[...])
        upstream = upstream * gate_column(gates, s_ref[0], number)
        gate_grad = upstream * up_part * sigmoid * (1.0 + gate_part * (1.0 - sigmoid))
        grad_ref[:, head(i)] = gate_grad.astype(BF)
        grad_ref[:, head(3 + i)] = (upstream * silu).astype(BF)
    grad = grad_ref[...]
    total[:, :HALF] += nt(grad, up0[...])
    total[:, HALF:] += nt(grad, up1[...])

    @pl.when(step == STEPS - 1)
    def _():
        whole = products[...]
        high = whole.astype(BF).astype(F32)
        extra = high + pltpu.roll(whole - high, E, 1)
        part[:, :D] = total[...].astype(BF)
        part[:, D:] = extra.astype(BF)


def ffn_backward(s, rows, gates, gate_up, weights, far_rows):
    return run(
        ffn_backward_kernel,
        [shaped((ROUTES, WIDE)), shaped((ROUTES, UP))],
        [s, rows, gates, gate_up, weights[0], weights[1], weights[0], weights[1]],
        flops=2 * ROUTES * D * PIECE,
        in_specs=[SMEM, fixed(ROUTES, D), fixed(ROUTES, E), by_step(ROUTES, 2 * STEP)]
        + ffn_weight_specs(),
        out_specs=[fixed(ROUTES, WIDE), by_step(ROUTES, 2 * STEP)],
        grid=(STEPS,),
        scratch=[pltpu.VMEM((ROUTES, D), F32), pltpu.VMEM((ROUTES, HD), F32)],
        far_in=(1, 2, 3) if far_rows else (2, 3),
    )


def ffn_weights_kernel(rows, grad_rows, gate_up_grad, gated, *refs):
    step = pl.program_id(0)
    out = refs[-1]

    def store(total):
        if len(refs) > 1:
            total = total + refs[0][...].astype(F32)
        out[...] = total.astype(BF)

    @pl.when(step < 2)
    def _():
        store(tn(rows[...], gate_up_grad[...]))

    @pl.when(step == 2)
    def _():
        store(tn(grad_rows[...], gated[...]))


def ffn_weights(half, rows, grad_rows, gate_up_grad, gated, *other):
    cut = pl.BlockSpec((ROUTES, HALF), lambda j: (0, half))
    third = pl.BlockSpec((ROUTES, DOWN), lambda j: (0, jnp.minimum(j, 1)))
    return run(
        ffn_weights_kernel,
        [shaped((HALF, PIECE))],
        [rows, grad_rows, gate_up_grad, gated, *other],
        flops=2 * ROUTES * HALF * PIECE,
        in_specs=[cut, cut, third, fixed(ROUTES, DOWN)] + [by_step(HALF, DOWN)] * len(other),
        out_specs=[by_step(HALF, DOWN)],
        grid=(3,),
    )[0]


def mid_kernel(hidden, gain, *refs):
    mid_ref, normed_ref, copies = refs[-3:]
    mid = hidden[...].astype(F32) + add_up(refs[:-3])
    mid_ref[...] = mid
    normed = (mid * rms_factor(mid) * gain[...]).astype(BF)
    normed_ref[...] = normed
    for index in range(8):
        copies[block(index), :] = normed


def last_kernel(mid, total, out):
    out[...] = (mid[...] + total[...].astype(F32)).astype(BF)


def result_kernel(mid, got, *outs):
    result = (mid[...] + add_blocks(got)).astype(BF)
    for out in outs:
        out[...] = result


def mid_backward_kernel(mid, own_gates, out_grad, gain, router, normed, got, *refs):
    mid_grad_ref, low_ref, small = refs
    total = add_blocks(got)
    extra = total[:, D:]
    gate_grad = (extra + pltpu.roll(extra, HD - E, 1))[:, :E]
    own = own_gates[...]
    logits_grad = own * (gate_grad - jnp.sum(own * gate_grad, axis=1, keepdims=True))
    logits_grad = logits_grad.astype(BF)
    upstream = total[:, :D] + nn(logits_grad, router[...])
    small[...] = jnp.zeros_like(small)
    grad, small[1:2, :] = norm_backward(mid[...], gain[...], upstream)
    small[2 : 2 + E, :] = tn(logits_grad, normed[...])
    mid_grad = out_grad[...].astype(F32) + grad
    mid_grad_ref[...] = mid_grad
    low_ref[...] = mid_grad.astype(BF)


def hidden_backward_kernel(hidden, gain, mid_grad, small_in, *refs):
    out, small, copies = refs[-3:]
    small[...] = small_in[...]
    grad, small[0:1, :] = norm_backward(hidden[...].astype(F32), gain[...], add_up(refs[:-3]))
    low = (mid_grad[...] + grad).astype(BF)
    out[...] = low
    for index in range(8):
        copies[block(index), :] = low


def small_forward_kernel(own, other, out):
    out[:, :HALF] = own[...].astype(F32).T[:64]
    out[:, HALF:] = other[...].astype(F32).T[:64]


def small_backward_kernel(first, second, own, other, both):
    both[...] = jnp.zeros_like(both)
    both[:SMALL, :] = first[...]
    both[32 : 32 + SMALL, :] = second[...]
    own[...] = both[:, :HALF].T.astype(BF)
    other[...] = both[:, HALF:].T.astype(BF)


def pack_kernel(s_ref, ffn0, ffn1, att1, *refs):
    outs = refs[4:]
    total = add_up(refs[:4])
    att0, small = total[:, :ATT].astype(BF), total[:, ATT:]
    smalls = (small.astype(BF), pltpu.roll(small, HD - 32, 1).astype(BF))
    for layer, ffn, att in ((0, ffn0, att0), (1, ffn1, att1[...])):
        for index in (0, 1):
            cut = slice(index * DBLK, (index + 1) * DBLK)
            for mine in (0, 1):

                @pl.when((s_ref[0] == layer) == (mine == 0))
                def _(out=outs[2 * mine + index]):
                    out[:, :PIECE] = ffn[cut, :]
                    out[:, PIECE : PIECE + ATT] = att[cut]
                    out[:, PIECE + ATT :] = smalls[layer][cut]


def final_kernel(s_ref, own, beside, straight, across, *outs):
    query, key, value, out, shared_in, shared_down, expert_in, expert_down, small = outs
    mine = own[...].astype(F32) + beside[...].astype(F32)
    theirs = straight[...].astype(F32) + across[...].astype(F32)
    att = mine[:, PIECE:] + theirs[:, PIECE:]
    query[...] = att[:, : GROUPS * HD]
    key[...] = att[:, KEYS]
    value[...] = att[:, VALUES]
    out[...] = att[:, QKV:ATT]
    small[...] = att[:, ATT:]
    for half in (0, 1):
        part = jnp.where(s_ref[0] == half, mine, theirs)
        for number in range(BLOCKS):
            at = number // 3 * 2 * STEP + number % 3 * HD
            gate_part, up_part = part[:, at : at + HD], part[:, at + STEP : at + STEP + HD]
            down = part[:, UP + number * HD : UP + (number + 1) * HD]
            if number < HALF_E:
                expert = half * HALF_E + number
                expert_in[:, head(2 * expert)] = gate_part
                expert_in[:, head(2 * expert + 1)] = up_part
                expert_down[expert] = down
            else:
                shared_in[:, head(half)] = gate_part
                shared_in[:, head(2 + half)] = up_part
                shared_down[:, head(half)] = down


def swap_core(part):
    return move(part, CORE, lambda c: (1 - c,))


def sum_row(part):
    return lax.psum_scatter(part, "z", scatter_dimension=0, tiled=True)


def gather_row(part):
    return lax.all_gather(part, "z", axis=0, tiled=True)


def per_device(
    tokens,
    cotangent,
    route_experts,
    route_slots,
    gain_attn,
    w_query,
    w_key,
    w_value,
    w_out,
    gain_ffn,
    w_router,
    w_shared_in,
    w_shared_down,
    w_expert_in,
    w_expert_down,
):
    s = lax.axis_index("section")
    xhi = lax.axis_index("xhi")
    core = lax.axis_index("core")
    z = lax.axis_index("z")
    t = lax.axis_index("tensor")
    first = s == 0
    s_arg = s.astype(jnp.int32)[None]
    t_arg = t.astype(jnp.int32)[None]

    small = jnp.concatenate([gain_attn[0][:, None], gain_ffn[0][:, None], w_router[0]], axis=1)
    small = jnp.pad(small, ((0, 0), (0, HD - 2 - E)))
    small = rolled(jnp.stack(tensor_gather(small)), (4 - t) % 4).reshape(DBLK, HD)
    att_piece = jnp.concatenate([w_query[0], w_key[0], w_value[0], w_out[0].T], axis=1)

    expert_in = w_expert_in[0].reshape(DBLK, 2, HALF_E, 2, HD)
    shared_in = w_shared_in[0].reshape(DBLK, 2, 2, HD)
    expert_down = w_expert_down[0].transpose(2, 0, 1).reshape(DBLK, 2, HALF_E * HD)
    shared_down = w_shared_down[0].T.reshape(DBLK, 2, HD)

    def ffn_piece(part):
        up = jnp.concatenate([expert_in[:, part], shared_in[:, None, :, part]], axis=1)
        up = up.reshape(DBLK, STEPS, 3, 2, HD).swapaxes(2, 3).reshape(DBLK, UP)
        return jnp.concatenate([up, expert_down[:, part], shared_down[:, part]], axis=1)

    ffn_own = jnp.where(first, ffn_piece(0), ffn_piece(1))
    ffn_other = jnp.where(first, ffn_piece(1), ffn_piece(0))

    place = jnp.arange(D, dtype=jnp.int32)
    at_core = (place // HALF + core) % 2
    at_z = (place // (2 * DBLK)) % 4
    at_x = (place // DBLK + xhi) % 2
    column = at_x * HALF + at_z * (2 * DBLK) + at_core * DBLK + place % DBLK
    order = (place[:, None] == column[None, :]).astype(BF)

    own_tokens = lax.dynamic_index_in_dim(tokens, s, 0, keepdims=False)
    own_rows = nn(own_tokens, order).astype(BF)
    grad_rows = lax.all_gather(cotangent.reshape(2 * ROWS, D), "tensor", axis=0, tiled=True)

    named = jnp.sum((route_experts[0][:, :, :, None] == jnp.arange(E)).astype(F32), axis=2)
    named = named.astype(BF).reshape(ROUTES, E)
    named_else = move(named, SECTION, lambda s: (s + 1,))
    small, own_rows = together(small, own_rows)

    att_beside = move(att_piece, SIDE, lambda s, x: (s, x + 1))
    att_straight = move(att_piece, SIDE, lambda s, x: (s + 1, x))
    att_across = move(att_piece, SIDE, lambda s, x: (s + 1, x + 1))
    small_x = [
        small,
        move(small, SIDE, lambda s, x: (s, x + 1)),
        move(small, SIDE, lambda s, x: (s + 1, x)),
        move(small, SIDE, lambda s, x: (s + 1, x + 1)),
    ]
    att_straight, small_x, ffn_own, ffn_other = together(att_straight, small_x, ffn_own, ffn_other)
    att_same = jnp.concatenate([att_piece, att_beside], axis=0)
    att_else = jnp.concatenate([att_straight, att_across], axis=0)
    att_pairs = [jnp.where(first, att_same, att_else), jnp.where(first, att_else, att_same)]
    ffn_straight = move(ffn_other, SIDE, lambda s, x: (s + 1, x))
    ffn_across = move(ffn_other, SIDE, lambda s, x: (s + 1, x + 1))
    ffn_beside0 = move(ffn_own, SIDE, lambda s, x: (s, x + 1), lambda s, x: s == 0)

    small_same = jnp.concatenate(small_x[:2], axis=0)[:, :32]
    small_else = jnp.concatenate(small_x[2:], axis=0)[:, :32]
    att_pair0 = jnp.concatenate(
        [
            att_pairs[0],
            jnp.where(first, small_same, small_else),
            jnp.where(first, small_else, small_same),
            jnp.zeros((2 * DBLK, HD - 64), BF),
        ],
        axis=1,
    )
    att_pair1 = att_pairs[1]
    att_pair0, grad_rows, named_else = together(att_pair0, grad_rows, named_else)
    masks = [jnp.where(s == layer, named, named_else).astype(F32) for layer in (0, 1)]
    att_row0 = gather_row(att_pair0)

    hidden_blocks = tensor_gather(own_rows)
    grad_rows = nn(grad_rows, order).astype(BF)
    grad_rows = grad_rows.reshape(4, 2, ROWS, D).swapaxes(0, 1).reshape(ROUTES, D)
    own_cotangent = lax.dynamic_slice_in_dim(grad_rows, (4 * s + t) * ROWS, ROWS, 0)

    from_x = (ffn_straight, ffn_across, ffn_beside0)
    from_x, hidden_blocks, att_row0 = together(from_x, hidden_blocks, att_row0)
    ffn_straight, ffn_across, ffn_beside0 = from_x
    ffn_else = jnp.concatenate([ffn_straight, ffn_across], axis=0)
    ffn_pair0 = jnp.where(first, jnp.concatenate([ffn_own, ffn_beside0], axis=0), ffn_else)
    ffn_pair0, hidden_blocks = together(ffn_pair0, hidden_blocks)
    ffn_row0 = gather_row(ffn_pair0)
    att_w = [(att_row0, swap_core(att_row0)), None]
    small = run(
        small_forward_kernel,
        [shaped((64, D), F32)],
        att_w[0],
        in_specs=[pl.BlockSpec((HALF, HD), lambda i: (0, ATT // HD))] * 2,
        out_specs=[pl.BlockSpec((64, D), lambda i: (0, 0))],
        grid=(1,),
    )[0]
    ffn_w = [None, None]
    kept = []
    for layer in (0, 1):
        at = 32 * layer
        attn_gain, ffn_gain = small[at : at + 1], small[at + 1 : at + 2]
        router = small[at + 2 : at + 2 + E].astype(BF)
        parts, att_saved = attention_forward(t_arg, hidden_blocks, attn_gain, att_w[layer])
        normed, *att_saved = att_saved
        mid, normed_ffn, copies = run(
            mid_kernel,
            [shaped((ROWS, D), F32), shaped((ROWS, D)), shaped((ROUTES, D))],
            [hidden_blocks[0], ffn_gain, parts[0], *tensor_send(parts)],
            far_out=(1,),
        )
        rows = group_exchange(copies)
        if layer == 0:
            normed, ffn_own = together(normed, ffn_own)
            ffn_beside1 = move(ffn_own, SIDE, lambda s, x: (s, x + 1), lambda s, x: s == 1)
            ffn_pair1 = jnp.where(first, ffn_else, jnp.concatenate([ffn_own, ffn_beside1], axis=0))
            ffn_row0, rows, att_pair1, ffn_pair1 = together(ffn_row0, rows, att_pair1, ffn_pair1)
            ffn_w[0] = (ffn_row0, swap_core(ffn_row0))
            att_row1 = gather_row(att_pair1)
            ffn_row1 = gather_row(ffn_pair1)
        else:
            ffn_row1, mid = together(ffn_row1, mid)
            ffn_w[1] = (ffn_row1, swap_core(ffn_row1))
        part, gates, own_gates, gate_up, gated = ffn_forward(
            s_arg, t_arg, rows, router, masks[layer], ffn_w[layer]
        )
        if layer == 1:
            sum1 = lax.psum_scatter(part, GROUP, scatter_dimension=0, tiled=True)
        kept.append((hidden_blocks[0], attn_gain, normed, *att_saved))
        kept.append((mid, ffn_gain, router, normed_ffn, rows, gates, own_gates, gate_up, gated))
        if layer == 0:
            outs = [shaped((ROWS, D))] * 2
            own_result, result = run(result_kernel, outs, [mid, group_exchange(part)])
            hidden_blocks = tensor_gather(own_result)
            att_row1, result = together(att_row1, result)
            att_w[1] = (att_row1, swap_core(att_row1))

    in_grads = [None, None]
    small_grads = [None, None]
    ffn_sums = [None, None]
    att_sums = [None, None]
    out_low = own_cotangent
    for layer in (1, 0):
        hidden, attn_gain, normed, qkv, probs, attended = kept[2 * layer]
        mid, ffn_gain, router, normed_ffn, rows, gates, own_gates, gate_up, gated = kept[2 * layer + 1]
        if layer == 0:
            gated, sum1 = together(gated, sum1)
        part_grad, gate_up_grad = ffn_backward(
            s_arg, grad_rows, gates, gate_up, ffn_w[layer], layer == 1
        )
        ffn_parts = (rows, grad_rows, gate_up_grad, gated)
        got = group_exchange(part_grad)
        own = ffn_weights(0, *ffn_parts, swap_core(ffn_weights(1, *ffn_parts)))
        got, own = together(got, own)
        if layer == 0:
            own, ffn_sums[1] = together(own, ffn_sums[1])
        ffn_sums[layer] = sum_row(own)
        mid_grad, mid_low, small = run(
            mid_backward_kernel,
            [shaped((ROWS, D), F32), shaped((ROWS, D)), shaped((SMALL, D), F32)],
            [mid, own_gates, out_low, ffn_gain, router, normed_ffn, got],
            far_in=(0, 1, 2, 3, 4, 5),
            far_out=(0, 2),
        )
        mid_blocks = tensor_gather(mid_low)
        parts, mid_rows, qkv_grad = attention_backward(mid_blocks, att_w[layer], qkv, probs)
        got = tensor_send(parts)
        att_parts = (normed, mid_rows, qkv_grad, attended)
        att_other = attention_weights(1, *att_parts)
        att_own = attention_weights(0, *att_parts, swap_core(att_other))
        if layer == 1:
            *got, att_other = together(*got, att_other)
        else:
            *got, att_own = together(*got, att_own)
        out_low, small_grads[layer], copies = run(
            hidden_backward_kernel,
            [shaped((ROWS, D)), shaped((SMALL, D), F32), shaped((ROUTES, D))],
            [hidden, attn_gain, mid_grad, small, parts[0], *got],
            far_in=(0, 1, 2, 3),
            far_out=(0, 1),
        )
        in_grads[layer] = out_low
        if layer == 1:
            grad_rows, att_own = together(group_exchange(copies), att_own)
            att_sums[1] = sum_row(att_own)
    def spread_z(part):
        blocks = rolled(part.reshape(4, 2 * DBLK, -1), z)
        return [blocks[0]] + [move(blocks[k], ROW, lambda at, k=k: (at + k,)) for k in (1, 2, 3)]

    small_own, small_other = run(
        small_backward_kernel,
        [shaped((HALF, HD))] * 2,
        small_grads,
        scratch=[pltpu.VMEM((HD, D), F32)],
    )
    small_own = (small_own.astype(F32) + swap_core(small_other).astype(F32)).astype(BF)
    att_blocks = spread_z(jnp.concatenate([att_own, small_own], axis=1))
    result1 = run(last_kernel, [shaped((ROWS, D))], [kept[3][0], sum1])[0]

    same0, same1, other0, other1 = run(
        pack_kernel,
        [shaped((DBLK, PIECE + ATT_PAD))] * 4,
        [s_arg, *ffn_sums, att_sums[1], *att_blocks],
        1,
        far_in=(1, 2, 3),
    )
    beside = move(same1, SIDE, lambda s, x: (s, x + 1))
    straight = move(other0, SIDE, lambda s, x: (s + 1, x))
    across = move(other1, SIDE, lambda s, x: (s + 1, x + 1))
    grads = run(
        final_kernel,
        [
            shaped(shape, F32)
            for shape in (
                (DBLK, GROUPS * HD),
                (DBLK, HD),
                (DBLK, HD),
                (DBLK, GROUPS * HD),
                (DBLK, 4 * HD),
                (DBLK, 2 * HD),
                (DBLK, 2 * E * HD),
                (E, DBLK, HD),
                (DBLK, HD),
            )
        ],
        [s_arg, same0, beside, straight, across],
        1,
    )
    grad_query, grad_key, grad_value, grad_out, grad_shared_in, grad_shared_down = grads[:6]
    grad_expert_in, grad_expert_down, small = grads[6:]

    def both_sequences(values):
        low = nt(jnp.concatenate(values, axis=0), order).astype(BF).reshape(2, ROWS, D)
        mine = jnp.where(first, low[0], low[1])
        got = move(jnp.where(first, low[1], low[0]), SECTION, lambda s: (s + 1,))
        return jnp.where(first, jnp.stack([mine, got]), jnp.stack([got, mine]))[None]

    values_out = both_sequences([result, result1])
    grads_in = both_sequences(in_grads)

    small = rolled(small.reshape(4, DBLK // 4, HD), t)
    small_sum = small[0]
    for got in tensor_send([small[k] for k in range(4)]):
        small_sum = small_sum + got

    return (
        values_out,
        grads_in,
        small_sum[:, 0][None],
        grad_query[None],
        grad_key[None],
        grad_value[None],
        grad_out.T[None],
        small_sum[:, 1][None],
        small_sum[:, 2 : 2 + E][None],
        grad_shared_in.reshape(1, DBLK, 2, 2 * HD),
        grad_shared_down.T[None],
        grad_expert_in.reshape(1, DBLK, E, 2, HD),
        grad_expert_down.swapaxes(1, 2)[None],
    )


def solution(mesh):
    split = Mesh(
        mesh.devices.reshape(2, 2, 4, 2, 4), ("section", "xhi", "z", "core", "tensor")
    )
    dp = ("xhi", "z", "core")
    both = dp + ("tensor",)
    placed = (
        P(dp, "tensor", None),
        P(dp, "tensor", None),
        P("section", dp, None, None),
        P("section", dp, None, None),
        P("section", both),
        P("section", dp, "tensor"),
        P("section", dp, "tensor"),
        P("section", dp, "tensor"),
        P("section", "tensor", dp),
        P("section", both),
        P("section", both, None),
        P("section", dp, None, "tensor"),
        P("section", "tensor", dp),
        P("section", dp, None, None, "tensor"),
        P("section", None, "tensor", dp),
    )
    return jax.shard_map(
        per_device,
        mesh=split,
        in_specs=placed,
        out_specs=(
            P("section", dp, "tensor", None),
            P("section", dp, "tensor", None),
            P("section", both),
            P("section", dp, "tensor"),
            P("section", dp, "tensor"),
            P("section", dp, "tensor"),
            P("section", "tensor", dp),
            P("section", both),
            P("section", both, None),
            P("section", dp, None, "tensor"),
            P("section", "tensor", dp),
            P("section", dp, None, None, "tensor"),
            P("section", None, "tensor", dp),
        ),
        check_vma=False,
    )
```
